32 devices in a mesh: ctx: 8 (over z, x), dec: 4 (over y, core).
Axes of the slice: x: 2, y: 2, z: 4, core: 2. Of those that a mesh axis runs over, the one named last changes fastest.
Arguments:
- queries: bfloat16 [64, 2, 8192], P(('ctx', 'dec')), may hold values from -256 to 256
- prompt_keys: bfloat16 [16384, 8, 128], P('ctx', 'dec'), may hold values from -40 to 40
- prompt_values: bfloat16 [16384, 8, 128], P('ctx', 'dec'), may hold values from -6 to 6
- suffix_keys: bfloat16 [64, 1024, 8, 128], P(('ctx', 'dec')), may hold values from -22 to 22
- suffix_values: bfloat16 [64, 1024, 8, 128], P(('ctx', 'dec')), may hold values from -6 to 6
- new_keys: bfloat16 [64, 2, 8, 128], P(('ctx', 'dec')), may hold values from -36 to 36
- new_values: bfloat16 [64, 2, 8, 128], P(('ctx', 'dec')), may hold values from -6 to 6
- lengths: int32 [64], P(('ctx', 'dec')), may hold values from 1 to 1024, as said below
Outputs:
- attended: bfloat16 [64, 2, 8192], P(('ctx', 'dec'))
The draws below stay inside these ranges and needn't reach their ends.
Inputs may be any that keep to these rules, and one draw needn't show every extreme that they name: `lengths`: at least one sample has exactly 1024 cached suffix tokens in every draw.
All inputs are finite; a program needn't handle non-finite values.
Results may differ from the reference program's by a relative error of at most 0.003.
Values may be sent and summed in bfloat16 or wider, within the bound.
A program may use at most 128 MiB of HBM per device.

```python
import jax
import jax.numpy as jnp
from jax import lax

HQ = 64
KVH = 8
HD = 128
STEPS = 2
PBLK = 2048
SUF = 1024
PROMPT = 16384
SAMPLES = 64


def shared_normals(key):
    return jax.random.normal(jax.random.fold_in(key, 11), (PROMPT, KVH, HD), jnp.float32)


def draw_prompt_keys(key, part):
    return (3.0 * shared_normals(key)).astype(jnp.bfloat16)


def draw_queries(key, part):
    folded = jax.random.fold_in(key, 5)
    drawn = jax.random.normal(folded, (SAMPLES, STEPS, HQ * HD), jnp.float32)
    return drawn.astype(jnp.bfloat16)


def draw_lengths(key, part):
    key = jax.random.fold_in(key, 7)
    first_key, second_key = jax.random.split(key)
    drawn_lengths = jax.random.randint(first_key, (SAMPLES,), 1, SUF + 1, dtype=jnp.int32)
    chosen = jax.random.randint(second_key, (), 0, SAMPLES, dtype=jnp.int32)
    return jnp.where(jnp.arange(SAMPLES, dtype=jnp.int32) == chosen, jnp.int32(SUF), drawn_lengths)


def level_of(own_key, extent, cuts, low, top_value):
    level = 1.0
    for dim, parts in cuts:
        steps = jax.random.uniform(jax.random.fold_in(jax.random.fold_in(own_key, 6), dim), (parts,), jnp.float32, low / len(cuts), top_value / len(cuts))
        level = level * jnp.repeat(jnp.exp(steps), extent[dim] // parts).reshape((-1,) + (1,) * (len(extent) - 1 - dim))
    return level


def centred(rng, dims, scale, limit, cuts=(), kind=jnp.bfloat16):
    loudness = level_of(rng, dims, cuts, -0.22, 0.18) if cuts else 1.0
    values = jax.random.normal(rng, dims, jnp.float32) * scale * loudness
    return jnp.minimum(jnp.maximum(values, -limit), limit).astype(kind)


def setup_inputs(seed: int = 0) -> dict:
    key_list = jax.random.split(jax.random.key(seed), 9)
    queries = draw_queries(jax.random.fold_in(key_list[8], 71), 0)
    prompt_keys = draw_prompt_keys(jax.random.fold_in(key_list[8], 71), 0)
    prompt_values = centred(key_list[2], (PROMPT, KVH, HD), 1.0, 6.0, ((0, 8), (1, 4)))
    suffix_keys = centred(key_list[3], (SAMPLES, SUF, KVH, HD), 3.8, 22.0, ((0, 32),))
    suffix_values = centred(key_list[4], (SAMPLES, SUF, KVH, HD), 1.0, 6.0, ((0, 32),))
    new_keys = centred(key_list[5], (SAMPLES, STEPS, KVH, HD), 6.0, 36.0, ((0, 32),))
    new_values = centred(key_list[6], (SAMPLES, STEPS, KVH, HD), 1.0, 6.0, ((0, 32),))
    lengths = draw_lengths(jax.random.fold_in(key_list[8], 71), 0)
    return dict(queries=queries, prompt_keys=prompt_keys, prompt_values=prompt_values, suffix_keys=suffix_keys, suffix_values=suffix_values, new_keys=new_keys, new_values=new_values, lengths=lengths)


MASKED_SCORE = -1.0e30


def block_part(scores, visible, values, form):
    masked = jnp.where(visible, scores, MASKED_SCORE)
    block_max = jnp.max(masked, axis=-1)
    weights = jnp.where(visible, jnp.exp(masked - block_max[..., None]), 0.0).astype(jnp.bfloat16)
    wide_weights = weights.astype(jnp.float32)
    block_total = jnp.sum(wide_weights, axis=-1)
    block_sum = jnp.einsum(form, wide_weights, values.astype(jnp.float32))
    return block_max, block_total, block_sum


def merge_parts(left, right):
    highest = jnp.maximum(left[0], right[0])
    left_factor = jnp.exp(left[0] - highest)
    right_factor = jnp.exp(right[0] - highest)
    return (highest, left[1] * left_factor + right[1] * right_factor,
            left[2] * left_factor[..., None] + right[2] * right_factor[..., None])


def reference(queries, prompt_keys, prompt_values, suffix_keys, suffix_values, new_keys, new_values, lengths):
    per_group = HQ // KVH
    inverse_root = HD ** -0.5
    grouped = queries.astype(jnp.float32).reshape(SAMPLES, STEPS, KVH, per_group, HD)
    state_shape = (SAMPLES, STEPS, KVH, per_group)
    running = (jnp.full(state_shape, MASKED_SCORE, jnp.float32), jnp.zeros(state_shape, jnp.float32),
               jnp.zeros(state_shape + (HD,), jnp.float32))
    key_span = min(512, PBLK)
    key_blocks = prompt_keys.reshape(PROMPT // key_span, key_span, KVH, HD)
    value_blocks = prompt_values.reshape(PROMPT // key_span, key_span, KVH, HD)

    def prompt_step(carried, blocks_pair):
        scores = jnp.einsum('stgqd,kgd->stgqk', grouped, blocks_pair[0].astype(jnp.float32)) * inverse_root
        return merge_parts(carried, block_part(scores, True, blocks_pair[1], 'stgqk,kgd->stgqd')), None

    running, _ = lax.scan(prompt_step, running, (key_blocks, value_blocks))
    suffix_span = min(512, SUF)

    def suffix_step(carried, number):
        offset = number * suffix_span
        keys_here = lax.dynamic_slice_in_dim(suffix_keys, offset, suffix_span, 1).astype(jnp.float32)
        values_here = lax.dynamic_slice_in_dim(suffix_values, offset, suffix_span, 1)
        scores = jnp.einsum('stgqd,skgd->stgqk', grouped, keys_here) * inverse_root
        positions = offset + jnp.arange(suffix_span, dtype=jnp.int32)
        visible = (positions[None, :] < lengths[:, None])[:, None, None, None, :]
        return merge_parts(carried, block_part(scores, visible, values_here, 'stgqk,skgd->stgqd')), None

    running, _ = lax.scan(suffix_step, running, jnp.arange(SUF // suffix_span, dtype=jnp.int32))
    scores = jnp.einsum('stgqd,sugd->stgqu', grouped, new_keys.astype(jnp.float32)) * inverse_root
    step_index = jnp.arange(STEPS, dtype=jnp.int32)
    visible = (step_index[None, :] <= step_index[:, None])[None, :, None, None, :]
    running = merge_parts(running, block_part(scores, visible, new_values, 'stgqu,sugd->stgqd'))
    attended = running[2] / running[1][..., None]
    return attended.astype(jnp.bfloat16).reshape(SAMPLES, STEPS, HQ * HD)
```

```python
import functools

import jax
import jax.numpy as jnp
from jax import lax
from jax.experimental import pallas as pl
from jax.experimental.pallas import tpu as pltpu
from jax.sharding import PartitionSpec as P

MESH = pl.DeviceIdType.MESH
MASKED_SCORE = -1e30
FLOOR = -1e29
LOG2E = 1.4426950408889634
F32 = jnp.float32
BF16 = jnp.bfloat16
NT = (((1,), (1,)), ((), ()))


def dot_nt(left, right):
    return lax.dot_general(left, right, NT, preferred_element_type=F32)


def dot(left, right):
    return jnp.dot(left, right, preferred_element_type=F32)


def kernel(
    sizes,
    q_ref,
    nk_ref,
    nv_ref,
    len_ref,
    pk_hbm,
    pv_hbm,
    sk_hbm,
    sv_hbm,
    out_ref,
    pk_raw,
    pv_raw,
    sk,
    sv,
    keys,
    values_t,
    place,
    qbuf,
    own_o,
    own_s,
    xo_send,
    xs_send,
    xo_recv,
    xs_recv,
    zo_send,
    zs_send,
    zo_recv,
    zs_recv,
    fo,
    fs,
    po_recv,
    ps_recv,
    stat_rows,
    suf_o,
    suf_m,
    suf_l,
    load_sem,
    g1_send,
    g1_recv,
    g2_send,
    g2_recv,
    gx_send,
    gx_recv,
    xo_sem,
    xs_sem,
    zo_sem,
    zs_sem,
    po_sem,
    ps_sem,
):
    ctx_n, dec_n, groups, rows, head_dim, kv_heads, per_group, steps, own = sizes
    pairs = ctx_n // 2
    unit = dec_n * rows
    positions = keys.shape[1]
    suffix_rows = sk.shape[1]
    scale = head_dim ** (-0.5) * LOG2E
    c = lax.axis_index("ctx")
    d = lax.axis_index("dec")
    z = c // 2
    x = c % 2

    def at_z(j, half):
        other = lax.bitwise_xor(z, jnp.int32(j))
        return other * 2 + (x if half == 0 else 1 - x)

    def dec_of(j):
        return lax.bitwise_xor(d, jnp.int32(j))

    loads = []
    for i, (src, dst) in enumerate(((pk_hbm, pk_raw), (pv_hbm, pv_raw))):
        loads.append(pltpu.make_async_copy(src, dst, load_sem.at[i]))
    for s in range(own):
        for i, (src, dst) in enumerate(((sk_hbm, sk), (sv_hbm, sv))):
            loads.append(pltpu.make_async_copy(src.at[s], dst.at[s], load_sem.at[2 + 2 * s + i]))
    for load in loads:
        load.start()

    barrier = pltpu.get_barrier_semaphore()
    partners = [(c, dec_of(j)) for j in range(1, dec_n)]
    partners += [(at_z(j, 0), d) for j in range(1, pairs)]
    partners += [(at_z(0, 1), d)]
    for partner in partners:
        pl.semaphore_signal(barrier, inc=1, device_id=partner, device_id_type=MESH)
    pl.semaphore_wait(barrier, len(partners))

    def remote(src, dst, send_sem, recv_sem, target):
        return pltpu.make_async_remote_copy(
            src_ref=src, dst_ref=dst, send_sem=send_sem, recv_sem=recv_sem,
            device_id=target, device_id_type=MESH,
        )

    own_rows = pl.ds(pl.multiple_of(d * rows, rows), rows)
    g1 = []
    for j in range(1, dec_n):
        copy = remote(q_ref.at[dec_of(j)], qbuf.at[c, :, own_rows, :],
                      g1_send.at[j], g1_recv.at[j], (c, dec_of(j)))
        copy.start()
        g1.append(copy)
    qbuf[c, :, own_rows, :] = q_ref[d]
    for copy in g1:
        copy.wait()
    g2 = {}
    for j in range(1, pairs):
        g2[j] = remote(qbuf.at[c], qbuf.at[c], g2_send.at[j], g2_recv.at[j], (at_z(j, 0), d))
        g2[j].start()
    gx = {}

    def forward(j):
        if j:
            g2[j].wait_recv()
        here = at_z(j, 0)
        gx[j] = remote(qbuf.at[here], qbuf.at[here], gx_send.at[j], gx_recv.at[j], (at_z(0, 1), d))
        gx[j].start()

    forward(0)

    span = 256 // groups
    perm_r = lax.broadcasted_iota(jnp.int32, (256, 256), 0)
    perm_i = lax.broadcasted_iota(jnp.int32, (256, 256), 1)
    perm = ((perm_r % span) * groups + perm_r // span == perm_i).astype(BF16)
    eye = (lax.broadcasted_iota(jnp.int32, (head_dim, head_dim), 0)
           == lax.broadcasted_iota(jnp.int32, (head_dim, head_dim), 1)).astype(BF16)
    loads[0].wait()
    loads[1].wait()

    def prepare(b, carry):
        raw = pl.ds(pl.multiple_of(b * 256, 256), 256)
        there = pl.ds(pl.multiple_of(b * span, span), span)
        key_rows = dot(perm, pk_raw[raw, :]).astype(BF16)
        value_rows = dot(perm, pv_raw[raw, :]).astype(BF16)
        turned = dot_nt(eye, value_rows).astype(BF16)
        for g in range(groups):
            keys[g, there, :] = key_rows[g * span:(g + 1) * span]
            values_t[g, :head_dim, there] = turned[:, g * span:(g + 1) * span]
        return carry

    lax.fori_loop(0, positions * groups // 256, prepare, 0)
    values_t[:, head_dim:, :] = jnp.ones_like(values_t[:, head_dim:, :])

    forward(1)

    chunk = min(512, suffix_rows // kv_heads) * kv_heads
    per_row = steps * per_group
    q_rows = kv_heads * per_row
    line = lax.broadcasted_iota(jnp.int32, (q_rows, chunk), 0) // per_row
    column = lax.broadcasted_iota(jnp.int32, (q_rows, chunk), 1)
    place[...] = jnp.where(column % kv_heads == line, column // kv_heads, 1 << 30)
    ones = jnp.ones((chunk, head_dim), BF16)

    def suffix(s):
        loads[2 + 2 * s].wait()
        loads[3 + 2 * s].wait()
        q = q_ref[:, :, s * per_row:(s + 1) * per_row, :].reshape(q_rows, head_dim)
        length = len_ref[s]

        def part(scores, visible, values, many):
            masked = jnp.where(visible, scores, MASKED_SCORE)
            top = jnp.maximum(jnp.max(masked, axis=1, keepdims=True), FLOOR)
            weights = jnp.exp2((masked - top) * scale).astype(BF16)
            return top, dot(weights, many), dot(weights, values)

        def merge(left, right):
            top = jnp.maximum(left[0], right[0])
            a = jnp.exp2((left[0] - top) * scale)
            b = jnp.exp2((right[0] - top) * scale)
            return top, left[1] * a + right[1] * b, left[2] * a + right[2] * b

        new_rows = steps * kv_heads
        col = lax.broadcasted_iota(jnp.int32, (q_rows, new_rows), 1)
        row = lax.broadcasted_iota(jnp.int32, (q_rows, new_rows), 0)
        seen = (col % kv_heads == row // per_row) & (col // kv_heads <= (row % per_row) // per_group)
        state = part(dot_nt(q, nk_ref[s]), seen, nv_ref[s], jnp.ones((new_rows, head_dim), BF16))
        for b in range(suffix_rows // chunk):
            here = slice(b * chunk, (b + 1) * chunk)
            visible = place[...] < length - b * (chunk // kv_heads)
            state = merge(state, part(dot_nt(q, sk[s, here, :]), visible, sv[s, here, :], ones))
        mine = slice(s * per_row, (s + 1) * per_row)
        shape = (kv_heads, per_row, head_dim)
        suf_o[:, mine, :] = state[2].reshape(shape)
        suf_l[:, mine, :] = state[1].reshape(shape)
        suf_m[:, mine, :] = jnp.broadcast_to(state[0] * scale, (q_rows, head_dim)).reshape(shape)

    suffix(0)
    for j in range(2, pairs):
        forward(j)
    for s in range(1, own):
        suffix(s)

    block = min(512, positions)

    def tile(j):
        mine, theirs = at_z(j, 0), at_z(j, 1)

        def group(g, carry):
            q = jnp.concatenate([qbuf[mine, g], qbuf[theirs, g]], axis=0)
            tops, sums = [], []
            for b in range(positions // block):
                here = slice(b * block, (b + 1) * block)
                scores = dot_nt(keys[g, here, :], q)
                top = jnp.max(scores, axis=0, keepdims=True)
                weights = jnp.exp2((scores - top) * scale).astype(BF16)
                tops.append(top * scale)
                sums.append(dot(values_t[g, :, here], weights))
            top = functools.reduce(jnp.maximum, tops)
            total = sum(one * jnp.exp2(m - top) for one, m in zip(sums, tops))
            stats = jnp.concatenate([
                jnp.broadcast_to(top, (4, 2 * unit)), total[head_dim:head_dim + 4]], axis=0)
            total = total[:head_dim]
            own_o[j, g] = total[:, :unit]
            own_s[j, g] = stats[:, :unit]
            xo_send[j, g] = total[:, unit:].astype(BF16)
            xs_send[j, g] = stats[:, unit:]
            return carry

        lax.fori_loop(0, groups, group, 0)

    xs = {}
    zs = {}

    def send_x(j):
        target = (at_z(0, 1), d)
        xs[j] = (
            remote(xo_send.at[j], xo_recv.at[j], xo_sem.at[0, j], xo_sem.at[1, j], target),
            remote(xs_send.at[j], xs_recv.at[j], xs_sem.at[0, j], xs_sem.at[1, j], target),
        )
        for copy in xs[j]:
            copy.start()

    def merged(parts):
        top = functools.reduce(jnp.maximum, [stats[0:1] for _, stats in parts])
        total, weight = 0.0, 0.0
        for sums, stats in parts:
            factor = jnp.exp2(stats[0:1] - top)
            total = total + sums.astype(F32) * factor
            weight = weight + stats[4:5] * factor
        width = top.shape[1]
        return total, jnp.concatenate(
            [jnp.broadcast_to(top, (4, width)), jnp.broadcast_to(weight, (4, width))], axis=0)

    def merge_x(j):
        for copy in xs[j]:
            copy.wait_recv()
        for g in range(groups):
            total, stats = merged([(own_o[j, g], own_s[j, g]), (xo_recv[j, g], xs_recv[j, g])])
            if j:
                zo_send[j, g] = total.astype(BF16)
                zs_send[j, g] = stats
            else:
                own_o[j, g] = total
                own_s[j, g] = stats
        if j:
            target = (at_z(j, 0), d)
            zs[j] = (
                remote(zo_send.at[j], zo_recv.at[j], zo_sem.at[0, j], zo_sem.at[1, j], target),
                remote(zs_send.at[j], zs_recv.at[j], zs_sem.at[0, j], zs_sem.at[1, j], target),
            )
            for copy in zs[j]:
                copy.start()

    order = list(range(1, pairs)) + [0]
    for i, j in enumerate(order):
        gx[j].wait_recv()
        tile(j)
        send_x(j)
        if i:
            merge_x(order[i - 1])
    merge_x(0)

    for j in range(1, pairs):
        for copy in zs[j]:
            copy.wait_recv()
    for g in range(groups):
        total, stats = merged([(own_o[0, g], own_s[0, g])]
                              + [(zo_recv[j, g], zs_recv[j, g]) for j in range(1, pairs)])
        fo[g] = total.T
        fs[g] = stats
    ps = []
    for j in range(1, dec_n):
        target = dec_of(j)
        there = pl.ds(pl.multiple_of(target * rows, rows), rows)
        ps.append(remote(fo.at[:, there, :], po_recv.at[d], po_sem.at[0, j], po_sem.at[1, j],
                         (c, target)))
        ps.append(remote(fs, ps_recv.at[d], ps_sem.at[0, j], ps_sem.at[1, j], (c, target)))
    for copy in ps:
        copy.start()
    po_recv[d] = fo[:, own_rows, :]
    ps_recv[d] = fs[...]
    for copy in ps:
        copy.wait_recv()
    flat = ps_recv[...].reshape(kv_heads * 8, unit)
    stat_rows[...] = flat.T
    picked = stat_rows[own_rows, :]
    for a in range(dec_n):
        for g in range(groups):
            h = a * groups + g
            top_p = picked[:, h * 8:h * 8 + 1]
            sum_p = picked[:, h * 8 + 4:h * 8 + 5]
            top = jnp.maximum(top_p, suf_m[h])
            left = jnp.exp2(top_p - top)
            right = jnp.exp2(suf_m[h] - top)
            result = (po_recv[a, g] * left + suf_o[h] * right) / (sum_p * left + suf_l[h] * right)
            out_ref[a, g] = result.astype(BF16)

    for copy in list(g2.values()) + list(gx.values()):
        copy.wait_send()
    for both in list(xs.values()) + list(zs.values()):
        for copy in both:
            copy.wait_send()
    for copy in ps:
        copy.wait_send()


def local(ctx_n, dec_n, queries, prompt_keys, prompt_values, suffix_keys, suffix_values,
          new_keys, new_values, lengths):
    own, steps, features = queries.shape
    positions, groups, head_dim = prompt_keys.shape
    suffix_length, kv_heads = suffix_keys.shape[1:3]
    per_group = features // (kv_heads * head_dim)
    rows = own * steps * per_group
    unit = dec_n * rows
    pairs = ctx_n // 2
    sent = (
        queries.reshape(own, steps, dec_n, groups, per_group, head_dim)
        .transpose(2, 3, 0, 1, 4, 5)
        .reshape(dec_n, groups, rows, head_dim)
    )
    suffix_rows = suffix_length * kv_heads
    q_rows = kv_heads * steps * per_group
    chunk = min(512, suffix_length) * kv_heads
    sizes = (ctx_n, dec_n, groups, rows, head_dim, kv_heads, per_group, steps, own)
    vmem = pl.BlockSpec(memory_space=pltpu.VMEM)
    anywhere = pl.BlockSpec(memory_space=pl.ANY)
    dma = pltpu.SemaphoreType.DMA
    moved = (pairs, groups, head_dim, unit)
    noted = (pairs, groups, 8, unit)
    result = pl.pallas_call(
        functools.partial(kernel, sizes),
        out_shape=jax.ShapeDtypeStruct((dec_n, groups, rows, head_dim), BF16),
        in_specs=[vmem, vmem, vmem, pl.BlockSpec(memory_space=pltpu.SMEM)] + [anywhere] * 4,
        out_specs=vmem,
        scratch_shapes=[
            pltpu.VMEM((positions * groups, head_dim), BF16),
            pltpu.VMEM((positions * groups, head_dim), BF16),
            pltpu.VMEM((own, suffix_rows, head_dim), BF16),
            pltpu.VMEM((own, suffix_rows, head_dim), BF16),
            pltpu.VMEM((groups, positions, head_dim), BF16),
            pltpu.VMEM((groups, head_dim + 16, positions), BF16),
            pltpu.VMEM((q_rows, chunk), jnp.int32),
            pltpu.VMEM((ctx_n, groups, unit, head_dim), BF16),
            pltpu.VMEM(moved, F32),
            pltpu.VMEM(noted, F32),
            pltpu.VMEM(moved, BF16),
            pltpu.VMEM(noted, F32),
            pltpu.VMEM(moved, BF16),
            pltpu.VMEM(noted, F32),
            pltpu.VMEM(moved, BF16),
            pltpu.VMEM(noted, F32),
            pltpu.VMEM(moved, BF16),
            pltpu.VMEM(noted, F32),
            pltpu.VMEM((groups, unit, head_dim), F32),
            pltpu.VMEM((groups, 8, unit), F32),
            pltpu.VMEM((dec_n, groups, rows, head_dim), F32),
            pltpu.VMEM((dec_n, groups, 8, unit), F32),
            pltpu.VMEM((unit, kv_heads * 8), F32),
            pltpu.VMEM((kv_heads, rows, head_dim), F32),
            pltpu.VMEM((kv_heads, rows, head_dim), F32),
            pltpu.VMEM((kv_heads, rows, head_dim), F32),
            dma((2 + 2 * own,)),
            dma((dec_n,)),
            dma((dec_n,)),
            dma((pairs,)),
            dma((pairs,)),
            dma((pairs,)),
            dma((pairs,)),
            dma((2, pairs)),
            dma((2, pairs)),
            dma((2, pairs)),
            dma((2, pairs)),
            dma((2, dec_n)),
            dma((2, dec_n)),
        ],
        compiler_params=pltpu.CompilerParams(
            collective_id=0, has_side_effects=True, vmem_limit_bytes=56 * 1024 * 1024
        ),
    )(
        sent,
        new_keys.reshape(own, steps * kv_heads, head_dim),
        new_values.reshape(own, steps * kv_heads, head_dim),
        lengths,
        prompt_keys.reshape(positions * groups, head_dim),
        prompt_values.reshape(positions * groups, head_dim),
        suffix_keys.reshape(own, suffix_rows, head_dim),
        suffix_values.reshape(own, suffix_rows, head_dim),
    )
    return (
        result.reshape(dec_n, groups, own, steps, per_group, head_dim)
        .transpose(2, 3, 0, 1, 4, 5)
        .reshape(own, steps, features)
    )


def solution(mesh):
    return jax.shard_map(
        functools.partial(local, mesh.shape["ctx"], mesh.shape["dec"]),
        mesh=mesh,
        in_specs=(
            P(("ctx", "dec"), None, None),
            P("ctx", "dec", None),
            P("ctx", "dec", None),
            P(("ctx", "dec"), None, None, None),
            P(("ctx", "dec"), None, None, None),
            P(("ctx", "dec"), None, None, None),
            P(("ctx", "dec"), None, None, None),
            P(("ctx", "dec")),
        ),
        out_specs=P(("ctx", "dec"), None, None),
        check_vma=False,
    )
```

```python
import functools

import jax
import jax.numpy as jnp
from jax import lax
from jax.experimental import pallas as pl
from jax.experimental.pallas import tpu as pltpu
from jax.sharding import PartitionSpec as P

MESH = pl.DeviceIdType.MESH
MASKED_SCORE = -1e30
FLOOR = -1e29
LOG2E = 1.4426950408889634
F32 = jnp.float32
BF16 = jnp.bfloat16
NT = (((1,), (1,)), ((), ()))


def dot_nt(left, right):
    return lax.dot_general(left, right, NT, preferred_element_type=F32)


def dot(left, right):
    return jnp.dot(left, right, preferred_element_type=F32)


def kernel(
    sizes,
    q_ref,
    nk_ref,
    nv_ref,
    len_ref,
    pk_hbm,
    pv_hbm,
    sk_hbm,
    sv_hbm,
    out_ref,
    pk_raw,
    pv_raw,
    sk,
    sv,
    keys,
    values_t,
    qbuf,
    own_o,
    own_s,
    xo_send,
    xs_send,
    xo_recv,
    xs_recv,
    zo_send,
    zs_send,
    zo_recv,
    zs_recv,
    fo,
    fs,
    po_recv,
    ps_recv,
    stat_rows,
    suf_o,
    suf_m,
    suf_l,
    load_sem,
    g1_send,
    g1_recv,
    g2_send,
    g2_recv,
    gx_send,
    gx_recv,
    xo_sem,
    xs_sem,
    zo_sem,
    zs_sem,
    po_sem,
    ps_sem,
):
    ctx_n, dec_n, groups, rows, head_dim, kv_heads, per_group, steps, own = sizes
    pairs = ctx_n // 2
    unit = dec_n * rows
    positions = keys.shape[1]
    suffix_rows = sk.shape[1]
    scale = head_dim ** (-0.5) * LOG2E
    c = lax.axis_index("ctx")
    d = lax.axis_index("dec")
    z = c // 2
    x = c % 2

    def at_z(j, half):
        other = lax.bitwise_xor(z, jnp.int32(j))
        return other * 2 + (x if half == 0 else 1 - x)

    def dec_of(j):
        return lax.bitwise_xor(d, jnp.int32(j))

    loads = []
    for i, (src, dst) in enumerate(((pk_hbm, pk_raw), (pv_hbm, pv_raw))):
        loads.append(pltpu.make_async_copy(src, dst, load_sem.at[i]))
    for s in range(own):
        for i, (src, dst) in enumerate(((sk_hbm, sk), (sv_hbm, sv))):
            loads.append(pltpu.make_async_copy(src.at[s], dst.at[s], load_sem.at[2 + 2 * s + i]))
    for load in loads:
        load.start()

    barrier = pltpu.get_barrier_semaphore()
    partners = [(c, dec_of(j)) for j in range(1, dec_n)]
    partners += [(at_z(j, 0), d) for j in range(1, pairs)]
    partners += [(at_z(0, 1), d)]
    for partner in partners:
        pl.semaphore_signal(barrier, inc=1, device_id=partner, device_id_type=MESH)
    pl.semaphore_wait(barrier, len(partners))

    def remote(src, dst, send_sem, recv_sem, target):
        return pltpu.make_async_remote_copy(
            src_ref=src, dst_ref=dst, send_sem=send_sem, recv_sem=recv_sem,
            device_id=target, device_id_type=MESH,
        )

    span = 256 // groups
    perm_r = lax.broadcasted_iota(jnp.int32, (256, 256), 0)
    perm_i = lax.broadcasted_iota(jnp.int32, (256, 256), 1)
    perm = ((perm_r % span) * groups + perm_r // span == perm_i).astype(BF16)
    eye = (lax.broadcasted_iota(jnp.int32, (head_dim, head_dim), 0)
           == lax.broadcasted_iota(jnp.int32, (head_dim, head_dim), 1)).astype(BF16)

    def prepare_keys(raw, there):
        key_rows = dot(perm, pk_raw[raw, :]).astype(BF16)
        for g in range(groups):
            keys[g, there, :] = key_rows[g * span:(g + 1) * span]

    def prepare_values(raw, there):
        value_rows = dot(perm, pv_raw[raw, :]).astype(BF16)
        turned = dot_nt(eye, value_rows).astype(BF16)
        for g in range(groups):
            values_t[g, :head_dim, there] = turned[:, g * span:(g + 1) * span]

    def prepare_all(prepare):
        count = positions * groups // 256
        at_once = 8

        def step(i, carry):
            for k in range(at_once):
                b = i * at_once + k
                prepare(pl.ds(pl.multiple_of(b * 256, 256), 256),
                        pl.ds(pl.multiple_of(b * span, span), span))
            return carry

        lax.fori_loop(0, count // at_once, step, 0)

    own_rows = pl.ds(pl.multiple_of(d * rows, rows), rows)
    g1 = []
    for j in range(1, dec_n):
        copy = remote(q_ref.at[:, :, dec_of(j)], qbuf.at[c, d],
                      g1_send.at[j], g1_recv.at[j], (c, dec_of(j)))
        copy.start()
        g1.append(copy)
    qbuf[c, d] = q_ref[:, :, d]
    loads[0].wait()
    prepare_all(prepare_keys)
    for copy in g1:
        copy.wait()
    g2 = {}
    for j in range(1, pairs):
        g2[j] = remote(qbuf.at[c], qbuf.at[c], g2_send.at[j], g2_recv.at[j], (at_z(j, 0), d))
        g2[j].start()
    gx = {}

    def forward(j):
        if j:
            g2[j].wait_recv()
        here = at_z(j, 0)
        gx[j] = remote(qbuf.at[here], qbuf.at[here], gx_send.at[j], gx_recv.at[j], (at_z(0, 1), d))
        gx[j].start()

    forward(0)

    loads[1].wait()
    prepare_all(prepare_values)
    values_t[:, head_dim:, :] = jnp.ones_like(values_t[:, head_dim:, :])

    forward(1)

    chunk = min(512, suffix_rows // kv_heads) * kv_heads
    per_step = kv_heads * per_group
    q_rows = steps * per_step
    per_row = steps * per_group
    lane_head = lax.broadcasted_iota(jnp.int32, (per_group, head_dim), 1) % kv_heads
    hits = [lane_head == g for g in range(kv_heads)]
    lane_place = lax.broadcasted_iota(jnp.int32, (per_row, head_dim), 1) // kv_heads

    def around(op, folded):
        shift = kv_heads
        while shift < head_dim:
            folded = op(folded, pltpu.roll(folded, shift, 1))
            shift *= 2
        return folded

    def by_row(folded):
        return jnp.concatenate(
            [folded[t * per_group:(t + 1) * per_group, g:g + 1]
             for t in range(steps) for g in range(kv_heads)], axis=0)

    def suffix(s):
        q = q_ref[s].astype(F32).reshape(q_rows, head_dim).astype(BF16)
        length = len_ref[s]

        def merge(left, right):
            top = jnp.maximum(left[0], right[0])
            a = jnp.exp2((left[0] - top) * scale)
            b = jnp.exp2((right[0] - top) * scale)
            return top, left[1] * a + right[1] * b, left[2] * a + right[2] * b

        new_rows = steps * kv_heads
        col = lax.broadcasted_iota(jnp.int32, (q_rows, new_rows), 1)
        row = lax.broadcasted_iota(jnp.int32, (q_rows, new_rows), 0)
        seen = (col % kv_heads == row // per_group % kv_heads) & (col // kv_heads <= row // per_step)
        masked = jnp.where(seen, dot_nt(q, nk_ref[s]), MASKED_SCORE)
        top = jnp.max(masked, axis=1, keepdims=True)
        weights = jnp.exp2((masked - top) * scale).astype(BF16)
        state = (top, jnp.sum(weights.astype(F32), axis=1, keepdims=True), dot(weights, nv_ref[s]))
        loads[2 + 2 * s].wait()
        loads[3 + 2 * s].wait()

        def part(b, state):
            here = pl.ds(pl.multiple_of(b * chunk, chunk), chunk)
            scores = dot_nt(q, sk[s, here, :])
            left = length - b * (chunk // kv_heads)
            found = []
            for k in range(chunk // head_dim):
                lanes = slice(k * head_dim, (k + 1) * head_dim)
                picked = []
                for t in range(steps):
                    base = t * per_step
                    one = scores[base:base + per_group, lanes]
                    for g in range(1, kv_heads):
                        first = base + g * per_group
                        one = jnp.where(hits[g], scores[first:first + per_group, lanes], one)
                    picked.append(one)
                visible = lane_place < left - k * (head_dim // kv_heads)
                found.append(jnp.where(visible, jnp.concatenate(picked, axis=0), MASKED_SCORE))
            top = jnp.maximum(around(jnp.maximum, functools.reduce(jnp.maximum, found)), FLOOR)
            total = 0.0
            spread = []
            for one in found:
                weights = jnp.exp2((one - top) * scale).astype(BF16).astype(F32)
                total = total + weights
                spread.append(jnp.concatenate(
                    [jnp.where(hits[g], weights[t * per_group:(t + 1) * per_group], 0.0)
                     for t in range(steps) for g in range(kv_heads)], axis=0).astype(BF16))
            summed = dot(jnp.concatenate(spread, axis=1), sv[s, here, :])
            return merge(state, (by_row(top), by_row(around(jnp.add, total)), summed))

        state = lax.fori_loop(0, suffix_rows // chunk, part, state)
        for t in range(steps):
            for g in range(kv_heads):
                first = t * per_step + g * per_group
                rows_here = slice(first, first + per_group)
                mine = slice(s * per_row + t * per_group, s * per_row + (t + 1) * per_group)
                shape = (per_group, head_dim)
                suf_o[g, mine, :] = state[2][rows_here]
                suf_l[g, mine, :] = jnp.broadcast_to(state[1][rows_here], shape)
                suf_m[g, mine, :] = jnp.broadcast_to(state[0][rows_here] * scale, shape)

    suffix(0)
    for j in range(2, pairs):
        forward(j)
    for s in range(1, own):
        suffix(s)

    block = min(512, positions)

    def tile(j):
        mine, theirs = at_z(j, 0), at_z(j, 1)

        for g in range(groups):
            q = jnp.concatenate(
                [qbuf[at, :, :, :, g].astype(F32).reshape(unit, head_dim) for at in (mine, theirs)],
                axis=0).astype(BF16)
            tops, sums = [], []
            for b in range(positions // block):
                here = slice(b * block, (b + 1) * block)
                scores = dot_nt(keys[g, here, :], q)
                top = jnp.max(scores, axis=0, keepdims=True)
                weights = jnp.exp2((scores - top) * scale).astype(BF16)
                tops.append(top * scale)
                sums.append(dot(values_t[g, :, here], weights))
            top = functools.reduce(jnp.maximum, tops)
            total = sum(one * jnp.exp2(m - top) for one, m in zip(sums, tops))
            stats = jnp.concatenate([
                jnp.broadcast_to(top, (4, 2 * unit)), total[head_dim:head_dim + 4]], axis=0)
            total = total[:head_dim]
            own_o[j, g] = total[:, :unit]
            own_s[j, g] = stats[:, :unit]
            xo_send[j, g] = total[:, unit:].astype(BF16)
            xs_send[j, g] = stats[:, unit:]

    xs = {}
    zs = {}

    def send_x(j):
        target = (at_z(0, 1), d)
        xs[j] = (
            remote(xo_send.at[j], xo_recv.at[j], xo_sem.at[0, j], xo_sem.at[1, j], target),
            remote(xs_send.at[j], xs_recv.at[j], xs_sem.at[0, j], xs_sem.at[1, j], target),
        )
        for copy in xs[j]:
            copy.start()

    def merged(parts):
        top = functools.reduce(jnp.maximum, [stats[0:1] for _, stats in parts])
        total, weight = 0.0, 0.0
        for sums, stats in parts:
            factor = jnp.exp2(stats[0:1] - top)
            total = total + sums.astype(F32) * factor
            weight = weight + stats[4:5] * factor
        width = top.shape[1]
        return total, jnp.concatenate(
            [jnp.broadcast_to(top, (4, width)), jnp.broadcast_to(weight, (4, width))], axis=0)

    def merge_x(j):
        for copy in xs[j]:
            copy.wait_recv()
        for g in range(groups):
            total, stats = merged([(own_o[j, g], own_s[j, g]), (xo_recv[j, g], xs_recv[j, g])])
            if j:
                zo_send[j, g] = total.astype(BF16)
                zs_send[j, g] = stats
            else:
                own_o[j, g] = total
                own_s[j, g] = stats
        if j:
            target = (at_z(j, 0), d)
            zs[j] = (
                remote(zo_send.at[j], zo_recv.at[j], zo_sem.at[0, j], zo_sem.at[1, j], target),
                remote(zs_send.at[j], zs_recv.at[j], zs_sem.at[0, j], zs_sem.at[1, j], target),
            )
            for copy in zs[j]:
                copy.start()

    order = list(range(1, pairs)) + [0]
    for i, j in enumerate(order):
        gx[j].wait_recv()
        tile(j)
        send_x(j)
        if i:
            merge_x(order[i - 1])
    merge_x(0)

    for j in range(1, pairs):
        for copy in zs[j]:
            copy.wait_recv()
    for g in range(groups):
        total, stats = merged([(own_o[0, g], own_s[0, g])]
                              + [(zo_recv[j, g], zs_recv[j, g]) for j in range(1, pairs)])
        fo[g] = total.T
        fs[g] = stats
    ps = []
    for j in range(1, dec_n):
        target = dec_of(j)
        there = pl.ds(pl.multiple_of(target * rows, rows), rows)
        ps.append(remote(fo.at[:, there, :], po_recv.at[d], po_sem.at[0, j], po_sem.at[1, j],
                         (c, target)))
        ps.append(remote(fs, ps_recv.at[d], ps_sem.at[0, j], ps_sem.at[1, j], (c, target)))
    for copy in ps:
        copy.start()
    po_recv[d] = fo[:, own_rows, :]
    ps_recv[d] = fs[...]
    for copy in ps:
        copy.wait_recv()
    flat = ps_recv[...].reshape(kv_heads * 8, unit)
    stat_rows[...] = flat.T
    picked = stat_rows[own_rows, :]
    for a in range(dec_n):
        for g in range(groups):
            h = a * groups + g
            top_p = picked[:, h * 8:h * 8 + 1]
            sum_p = picked[:, h * 8 + 4:h * 8 + 5]
            top = jnp.maximum(top_p, suf_m[h])
            left = jnp.exp2(top_p - top)
            right = jnp.exp2(suf_m[h] - top)
            result = (po_recv[a, g] * left + suf_o[h] * right) / (sum_p * left + suf_l[h] * right)
            for s in range(own):
                for t in range(steps):
                    first = (s * steps + t) * per_group
                    out_ref[s, t, a, g] = result[first:first + per_group].astype(BF16)

    for copy in list(g2.values()) + list(gx.values()):
        copy.wait_send()
    for both in list(xs.values()) + list(zs.values()):
        for copy in both:
            copy.wait_send()
    for copy in ps:
        copy.wait_send()


def local(ctx_n, dec_n, queries, prompt_keys, prompt_values, suffix_keys, suffix_values,
          new_keys, new_values, lengths):
    own, steps, features = queries.shape
    positions, groups, head_dim = prompt_keys.shape
    suffix_length, kv_heads = suffix_keys.shape[1:3]
    per_group = features // (kv_heads * head_dim)
    rows = own * steps * per_group
    unit = dec_n * rows
    pairs = ctx_n // 2
    by_head = (own, steps, dec_n, groups, per_group, head_dim)
    suffix_rows = suffix_length * kv_heads
    sizes = (ctx_n, dec_n, groups, rows, head_dim, kv_heads, per_group, steps, own)
    vmem = pl.BlockSpec(memory_space=pltpu.VMEM)
    anywhere = pl.BlockSpec(memory_space=pl.ANY)
    dma = pltpu.SemaphoreType.DMA
    moved = (pairs, groups, head_dim, unit)
    noted = (pairs, groups, 8, unit)
    result = pl.pallas_call(
        functools.partial(kernel, sizes),
        out_shape=jax.ShapeDtypeStruct(by_head, BF16),
        in_specs=[vmem, vmem, vmem, pl.BlockSpec(memory_space=pltpu.SMEM)] + [anywhere] * 4,
        out_specs=vmem,
        scratch_shapes=[
            pltpu.VMEM((positions * groups, head_dim), BF16),
            pltpu.VMEM((positions * groups, head_dim), BF16),
            pltpu.VMEM((own, suffix_rows, head_dim), BF16),
            pltpu.VMEM((own, suffix_rows, head_dim), BF16),
            pltpu.VMEM((groups, positions, head_dim), BF16),
            pltpu.VMEM((groups, head_dim + 16, positions), BF16),
            pltpu.VMEM((ctx_n, dec_n, own, steps, groups, per_group, head_dim), BF16),
            pltpu.VMEM(moved, F32),
            pltpu.VMEM(noted, F32),
            pltpu.VMEM(moved, BF16),
            pltpu.VMEM(noted, F32),
            pltpu.VMEM(moved, BF16),
            pltpu.VMEM(noted, F32),
            pltpu.VMEM(moved, BF16),
            pltpu.VMEM(noted, F32),
            pltpu.VMEM(moved, BF16),
            pltpu.VMEM(noted, F32),
            pltpu.VMEM((groups, unit, head_dim), F32),
            pltpu.VMEM((groups, 8, unit), F32),
            pltpu.VMEM((dec_n, groups, rows, head_dim), F32),
            pltpu.VMEM((dec_n, groups, 8, unit), F32),
            pltpu.VMEM((unit, kv_heads * 8), F32),
            pltpu.VMEM((kv_heads, rows, head_dim), F32),
            pltpu.VMEM((kv_heads, rows, head_dim), F32),
            pltpu.VMEM((kv_heads, rows, head_dim), F32),
            dma((2 + 2 * own,)),
            dma((dec_n,)),
            dma((dec_n,)),
            dma((pairs,)),
            dma((pairs,)),
            dma((pairs,)),
            dma((pairs,)),
            dma((2, pairs)),
            dma((2, pairs)),
            dma((2, pairs)),
            dma((2, pairs)),
            dma((2, dec_n)),
            dma((2, dec_n)),
        ],
        compiler_params=pltpu.CompilerParams(
            collective_id=0, has_side_effects=True, vmem_limit_bytes=56 * 1024 * 1024
        ),
    )(
        queries.reshape(by_head),
        new_keys.reshape(own, steps * kv_heads, head_dim),
        new_values.reshape(own, steps * kv_heads, head_dim),
        lengths,
        prompt_keys.reshape(positions * groups, head_dim),
        prompt_values.reshape(positions * groups, head_dim),
        suffix_keys.reshape(own, suffix_rows, head_dim),
        suffix_values.reshape(own, suffix_rows, head_dim),
    )
    return result.reshape(own, steps, features)


def solution(mesh):
    return jax.shard_map(
        functools.partial(local, mesh.shape["ctx"], mesh.shape["dec"]),
        mesh=mesh,
        in_specs=(
            P(("ctx", "dec"), None, None),
            P("ctx", "dec", None),
            P("ctx", "dec", None),
            P(("ctx", "dec"), None, None, None),
            P(("ctx", "dec"), None, None, None),
            P(("ctx", "dec"), None, None, None),
            P(("ctx", "dec"), None, None, None),
            P(("ctx", "dec")),
        ),
        out_specs=P(("ctx", "dec"), None, None),
        check_vma=False,
    )
```

```python
import functools

import jax
import jax.numpy as jnp
from jax import lax
from jax.experimental import pallas as pl
from jax.experimental.pallas import tpu as pltpu
from jax.sharding import PartitionSpec as P

MESH = pl.DeviceIdType.MESH
MASKED_SCORE = -1e30
FLOOR = -1e29
LOG2E = 1.4426950408889634
F32 = jnp.float32
BF16 = jnp.bfloat16
NT = (((1,), (1,)), ((), ()))


def dot_nt(left, right):
    return lax.dot_general(left, right, NT, preferred_element_type=F32)


def dot(left, right):
    return jnp.dot(left, right, preferred_element_type=F32)


def kernel(
    sizes,
    q_ref,
    nk_ref,
    nv_ref,
    len_ref,
    pk_hbm,
    pv_hbm,
    sk_hbm,
    sv_hbm,
    out_ref,
    pk_raw,
    pv_raw,
    sk,
    sv,
    keys,
    values_t,
    qbuf,
    own_o,
    own_s,
    xo_send,
    xs_send,
    xo_recv,
    xs_recv,
    zo_send,
    zs_send,
    zo_recv,
    zs_recv,
    fo,
    fs,
    po_recv,
    ps_recv,
    stat_rows,
    suf_o,
    suf_m,
    suf_l,
    load_sem,
    g1_send,
    g1_recv,
    g2_send,
    g2_recv,
    gx_send,
    gx_recv,
    xo_sem,
    xs_sem,
    zo_sem,
    zs_sem,
    po_sem,
    ps_sem,
):
    ctx_n, dec_n, groups, rows, head_dim, kv_heads, per_group, steps, own = sizes
    pairs = ctx_n // 2
    unit = dec_n * rows
    positions = keys.shape[1]
    suffix_rows = sk.shape[1]
    scale = head_dim ** (-0.5) * LOG2E
    c = lax.axis_index("ctx")
    d = lax.axis_index("dec")
    z = c // 2
    x = c % 2

    def at_z(j, half):
        other = lax.bitwise_xor(z, jnp.int32(j))
        return other * 2 + (x if half == 0 else 1 - x)

    def dec_of(j):
        return lax.bitwise_xor(d, jnp.int32(j))

    loads = []
    for i, (src, dst) in enumerate(((pk_hbm, pk_raw), (pv_hbm, pv_raw))):
        loads.append(pltpu.make_async_copy(src, dst, load_sem.at[i]))
    for s in range(own):
        for i, (src, dst) in enumerate(((sk_hbm, sk), (sv_hbm, sv))):
            loads.append(pltpu.make_async_copy(src.at[s], dst.at[s], load_sem.at[2 + 2 * s + i]))
    for load in loads:
        load.start()

    barrier = pltpu.get_barrier_semaphore()
    partners = [(c, dec_of(j)) for j in range(1, dec_n)]
    partners += [(at_z(j, 0), d) for j in range(1, pairs)]
    partners += [(at_z(0, 1), d)]
    for partner in partners:
        pl.semaphore_signal(barrier, inc=1, device_id=partner, device_id_type=MESH)
    pl.semaphore_wait(barrier, len(partners))

    def remote(src, dst, send_sem, recv_sem, target):
        return pltpu.make_async_remote_copy(
            src_ref=src, dst_ref=dst, send_sem=send_sem, recv_sem=recv_sem,
            device_id=target, device_id_type=MESH,
        )

    span = 256 // groups
    perm_r = lax.broadcasted_iota(jnp.int32, (256, 256), 0)
    perm_i = lax.broadcasted_iota(jnp.int32, (256, 256), 1)
    perm = ((perm_r % span) * groups + perm_r // span == perm_i).astype(BF16)
    eye = (lax.broadcasted_iota(jnp.int32, (head_dim, head_dim), 0)
           == lax.broadcasted_iota(jnp.int32, (head_dim, head_dim), 1)).astype(BF16)

    def prepare_keys(raw, there):
        key_rows = dot(perm, pk_raw[raw, :]).astype(BF16)
        for g in range(groups):
            keys[g, there, :] = key_rows[g * span:(g + 1) * span]

    def prepare_values(raw, there):
        value_rows = dot(perm, pv_raw[raw, :]).astype(BF16)
        turned = dot_nt(eye, value_rows).astype(BF16)
        for g in range(groups):
            values_t[g, :head_dim, there] = turned[:, g * span:(g + 1) * span]

    def prepare_all(prepare):
        count = positions * groups // 256
        at_once = 8

        def step(i, carry):
            for k in range(at_once):
                b = i * at_once + k
                prepare(pl.ds(pl.multiple_of(b * 256, 256), 256),
                        pl.ds(pl.multiple_of(b * span, span), span))
            return carry

        lax.fori_loop(0, count // at_once, step, 0)

    own_rows = pl.ds(pl.multiple_of(d * rows, rows), rows)
    g1 = []
    for j in range(1, dec_n):
        copy = remote(q_ref.at[:, :, dec_of(j)], qbuf.at[c, d],
                      g1_send.at[j], g1_recv.at[j], (c, dec_of(j)))
        copy.start()
        g1.append(copy)
    qbuf[c, d] = q_ref[:, :, d]
    loads[0].wait()
    prepare_all(prepare_keys)
    for copy in g1:
        copy.wait()
    g2 = {}
    for j in range(1, pairs):
        g2[j] = remote(qbuf.at[c], qbuf.at[c], g2_send.at[j], g2_recv.at[j], (at_z(j, 0), d))
        g2[j].start()
    gx = {}

    def forward(j):
        if j:
            g2[j].wait_recv()
        here = at_z(j, 0)
        gx[j] = remote(qbuf.at[here], qbuf.at[here], gx_send.at[j], gx_recv.at[j], (at_z(0, 1), d))
        gx[j].start()

    forward(0)

    loads[1].wait()
    prepare_all(prepare_values)
    values_t[:, head_dim:, :] = jnp.ones_like(values_t[:, head_dim:, :])

    forward(1)

    chunk = min(512, suffix_rows // kv_heads) * kv_heads
    per_step = kv_heads * per_group
    q_rows = steps * per_step
    per_row = steps * per_group
    lane_head = lax.broadcasted_iota(jnp.int32, (per_group, head_dim), 1) % kv_heads
    hits = [lane_head == g for g in range(kv_heads)]
    lane_place = lax.broadcasted_iota(jnp.int32, (per_row, head_dim), 1) // kv_heads

    def around(op, folded):
        shift = kv_heads
        while shift < head_dim:
            folded = op(folded, pltpu.roll(folded, shift, 1))
            shift *= 2
        return folded

    def by_row(folded):
        return jnp.concatenate(
            [folded[t * per_group:(t + 1) * per_group, g:g + 1]
             for t in range(steps) for g in range(kv_heads)], axis=0)

    def suffix(s):
        q = q_ref[s].astype(F32).reshape(q_rows, head_dim).astype(BF16)
        length = len_ref[s]

        def merge(left, right):
            top = jnp.maximum(left[0], right[0])
            a = jnp.exp2((left[0] - top) * scale)
            b = jnp.exp2((right[0] - top) * scale)
            return top, left[1] * a + right[1] * b, left[2] * a + right[2] * b

        new_rows = steps * kv_heads
        col = lax.broadcasted_iota(jnp.int32, (q_rows, new_rows), 1)
        row = lax.broadcasted_iota(jnp.int32, (q_rows, new_rows), 0)
        seen = (col % kv_heads == row // per_group % kv_heads) & (col // kv_heads <= row // per_step)
        masked = jnp.where(seen, dot_nt(q, nk_ref[s]), MASKED_SCORE)
        top = jnp.max(masked, axis=1, keepdims=True)
        weights = jnp.exp2((masked - top) * scale).astype(BF16)
        state = (top, jnp.sum(weights.astype(F32), axis=1, keepdims=True), dot(weights, nv_ref[s]))
        loads[2 + 2 * s].wait()
        loads[3 + 2 * s].wait()

        def part(b, state):
            here = pl.ds(pl.multiple_of(b * chunk, chunk), chunk)
            scores = dot_nt(q, sk[s, here, :])
            left = length - b * (chunk // kv_heads)
            found = []
            for k in range(chunk // head_dim):
                lanes = slice(k * head_dim, (k + 1) * head_dim)
                picked = []
                for t in range(steps):
                    base = t * per_step
                    one = scores[base:base + per_group, lanes]
                    for g in range(1, kv_heads):
                        first = base + g * per_group
                        one = jnp.where(hits[g], scores[first:first + per_group, lanes], one)
                    picked.append(one)
                visible = lane_place < left - k * (head_dim // kv_heads)
                found.append(jnp.where(visible, jnp.concatenate(picked, axis=0), MASKED_SCORE))
            top = jnp.maximum(around(jnp.maximum, functools.reduce(jnp.maximum, found)), FLOOR)
            total = 0.0
            spread = []
            for one in found:
                weights = jnp.exp2((one - top) * scale).astype(BF16).astype(F32)
                total = total + weights
                spread.append(jnp.concatenate(
                    [jnp.where(hits[g], weights[t * per_group:(t + 1) * per_group], 0.0)
                     for t in range(steps) for g in range(kv_heads)], axis=0).astype(BF16))
            summed = dot(jnp.concatenate(spread, axis=1), sv[s, here, :])
            return merge(state, (by_row(top), by_row(around(jnp.add, total)), summed))

        state = lax.fori_loop(0, suffix_rows // chunk, part, state)
        for t in range(steps):
            for g in range(kv_heads):
                first = t * per_step + g * per_group
                rows_here = slice(first, first + per_group)
                mine = slice(s * per_row + t * per_group, s * per_row + (t + 1) * per_group)
                shape = (per_group, head_dim)
                suf_o[g, mine, :] = state[2][rows_here]
                suf_l[g, mine, :] = jnp.broadcast_to(state[1][rows_here], shape)
                suf_m[g, mine, :] = jnp.broadcast_to(state[0][rows_here] * scale, shape)

    suffix(0)

    block = min(512, positions)

    def tile(j):
        mine, theirs = at_z(j, 0), at_z(j, 1)

        stages = [(g, b) for g in range(groups) for b in range(positions // block)]
        queries, tops, sums = {}, {}, {}
        for g in range(groups):
            queries[g] = jnp.concatenate(
                [qbuf[at, :, :, :, g].astype(F32).reshape(unit, head_dim) for at in (mine, theirs)],
                axis=0).astype(BF16)
            tops[g], sums[g] = [], []

        def score(g, b):
            return dot_nt(keys[g, b * block:(b + 1) * block, :], queries[g])

        def value(g, b, weights):
            sums[g].append(dot(values_t[g, :, b * block:(b + 1) * block], weights))

        def finish(g):
            top = functools.reduce(jnp.maximum, tops[g])
            total = sum(one * jnp.exp2(m - top) for one, m in zip(sums[g], tops[g]))
            stats = jnp.concatenate([
                jnp.broadcast_to(top, (4, 2 * unit)), total[head_dim:head_dim + 4]], axis=0)
            total = total[:head_dim]
            own_o[j, g] = total[:, :unit]
            own_s[j, g] = stats[:, :unit]
            xo_send[j, g] = total[:, unit:].astype(BF16)
            xs_send[j, g] = stats[:, unit:]

        scores = score(*stages[0])
        waiting = None
        for i, (g, b) in enumerate(stages):
            following = score(*stages[i + 1]) if i + 1 < len(stages) else None
            if waiting is not None:
                value(*waiting)
            top = jnp.max(scores, axis=0, keepdims=True)
            tops[g].append(top * scale)
            waiting = (g, b, jnp.exp2((scores - top) * scale).astype(BF16))
            scores = following
            if b == 0 and g:
                finish(g - 1)
        value(*waiting)
        finish(groups - 1)

    xs = {}
    zs = {}

    def send_x(j):
        target = (at_z(0, 1), d)
        xs[j] = (
            remote(xo_send.at[j], xo_recv.at[j], xo_sem.at[0, j], xo_sem.at[1, j], target),
            remote(xs_send.at[j], xs_recv.at[j], xs_sem.at[0, j], xs_sem.at[1, j], target),
        )
        for copy in xs[j]:
            copy.start()

    def merged(parts):
        top = functools.reduce(jnp.maximum, [stats[0:1] for _, stats in parts])
        total, weight = 0.0, 0.0
        for sums, stats in parts:
            factor = jnp.exp2(stats[0:1] - top)
            total = total + sums.astype(F32) * factor
            weight = weight + stats[4:5] * factor
        width = top.shape[1]
        return total, jnp.concatenate(
            [jnp.broadcast_to(top, (4, width)), jnp.broadcast_to(weight, (4, width))], axis=0)

    def merge_x(j):
        for copy in xs[j]:
            copy.wait_recv()
        for g in range(groups):
            total, stats = merged([(own_o[j, g], own_s[j, g]), (xo_recv[j, g], xs_recv[j, g])])
            if j:
                zo_send[j, g] = total.astype(BF16)
                zs_send[j, g] = stats
            else:
                own_o[j, g] = total
                own_s[j, g] = stats
        if j:
            target = (at_z(j, 0), d)
            zs[j] = (
                remote(zo_send.at[j], zo_recv.at[j], zo_sem.at[0, j], zo_sem.at[1, j], target),
                remote(zs_send.at[j], zs_recv.at[j], zs_sem.at[0, j], zs_sem.at[1, j], target),
            )
            for copy in zs[j]:
                copy.start()

    order = list(range(1, pairs)) + [0]
    for i, j in enumerate(order):
        if j and j + 1 < pairs:
            forward(j + 1)
        gx[j].wait_recv()
        tile(j)
        send_x(j)
        if i:
            merge_x(order[i - 1])
    for s in range(1, own):
        suffix(s)
    merge_x(0)

    for j in range(1, pairs):
        for copy in zs[j]:
            copy.wait_recv()
    for g in range(groups):
        total, stats = merged([(own_o[0, g], own_s[0, g])]
                              + [(zo_recv[j, g], zs_recv[j, g]) for j in range(1, pairs)])
        fo[g] = total.T
        fs[g] = stats
    ps = []
    for j in range(1, dec_n):
        target = dec_of(j)
        there = pl.ds(pl.multiple_of(target * rows, rows), rows)
        ps.append(remote(fo.at[:, there, :], po_recv.at[d], po_sem.at[0, j], po_sem.at[1, j],
                         (c, target)))
        ps.append(remote(fs, ps_recv.at[d], ps_sem.at[0, j], ps_sem.at[1, j], (c, target)))
    for copy in ps:
        copy.start()
    po_recv[d] = fo[:, own_rows, :]
    ps_recv[d] = fs[...]
    for copy in ps:
        copy.wait_recv()
    flat = ps_recv[...].reshape(kv_heads * 8, unit)
    stat_rows[...] = flat.T
    picked = stat_rows[own_rows, :]
    for a in range(dec_n):
        for g in range(groups):
            h = a * groups + g
            top_p = picked[:, h * 8:h * 8 + 1]
            sum_p = picked[:, h * 8 + 4:h * 8 + 5]
            top = jnp.maximum(top_p, suf_m[h])
            left = jnp.exp2(top_p - top)
            right = jnp.exp2(suf_m[h] - top)
            result = (po_recv[a, g] * left + suf_o[h] * right) / (sum_p * left + suf_l[h] * right)
            for s in range(own):
                for t in range(steps):
                    first = (s * steps + t) * per_group
                    out_ref[s, t, a, g] = result[first:first + per_group].astype(BF16)

    for copy in list(g2.values()) + list(gx.values()):
        copy.wait_send()
    for both in list(xs.values()) + list(zs.values()):
        for copy in both:
            copy.wait_send()
    for copy in ps:
        copy.wait_send()


def local(ctx_n, dec_n, queries, prompt_keys, prompt_values, suffix_keys, suffix_values,
          new_keys, new_values, lengths):
    own, steps, features = queries.shape
    positions, groups, head_dim = prompt_keys.shape
    suffix_length, kv_heads = suffix_keys.shape[1:3]
    per_group = features // (kv_heads * head_dim)
    rows = own * steps * per_group
    unit = dec_n * rows
    pairs = ctx_n // 2
    by_head = (own, steps, dec_n, groups, per_group, head_dim)
    suffix_rows = suffix_length * kv_heads
    sizes = (ctx_n, dec_n, groups, rows, head_dim, kv_heads, per_group, steps, own)
    vmem = pl.BlockSpec(memory_space=pltpu.VMEM)
    anywhere = pl.BlockSpec(memory_space=pl.ANY)
    dma = pltpu.SemaphoreType.DMA
    moved = (pairs, groups, head_dim, unit)
    noted = (pairs, groups, 8, unit)
    result = pl.pallas_call(
        functools.partial(kernel, sizes),
        out_shape=jax.ShapeDtypeStruct(by_head, BF16),
        in_specs=[vmem, vmem, vmem, pl.BlockSpec(memory_space=pltpu.SMEM)] + [anywhere] * 4,
        out_specs=vmem,
        scratch_shapes=[
            pltpu.VMEM((positions * groups, head_dim), BF16),
            pltpu.VMEM((positions * groups, head_dim), BF16),
            pltpu.VMEM((own, suffix_rows, head_dim), BF16),
            pltpu.VMEM((own, suffix_rows, head_dim), BF16),
            pltpu.VMEM((groups, positions, head_dim), BF16),
            pltpu.VMEM((groups, head_dim + 16, positions), BF16),
            pltpu.VMEM((ctx_n, dec_n, own, steps, groups, per_group, head_dim), BF16),
            pltpu.VMEM(moved, F32),
            pltpu.VMEM(noted, F32),
            pltpu.VMEM(moved, BF16),
            pltpu.VMEM(noted, F32),
            pltpu.VMEM(moved, BF16),
            pltpu.VMEM(noted, F32),
            pltpu.VMEM(moved, BF16),
            pltpu.VMEM(noted, F32),
            pltpu.VMEM(moved, BF16),
            pltpu.VMEM(noted, F32),
            pltpu.VMEM((groups, unit, head_dim), F32),
            pltpu.VMEM((groups, 8, unit), F32),
            pltpu.VMEM((dec_n, groups, rows, head_dim), F32),
            pltpu.VMEM((dec_n, groups, 8, unit), F32),
            pltpu.VMEM((unit, kv_heads * 8), F32),
            pltpu.VMEM((kv_heads, rows, head_dim), F32),
            pltpu.VMEM((kv_heads, rows, head_dim), F32),
            pltpu.VMEM((kv_heads, rows, head_dim), F32),
            dma((2 + 2 * own,)),
            dma((dec_n,)),
            dma((dec_n,)),
            dma((pairs,)),
            dma((pairs,)),
            dma((pairs,)),
            dma((pairs,)),
            dma((2, pairs)),
            dma((2, pairs)),
            dma((2, pairs)),
            dma((2, pairs)),
            dma((2, dec_n)),
            dma((2, dec_n)),
        ],
        compiler_params=pltpu.CompilerParams(
            collective_id=0, has_side_effects=True, vmem_limit_bytes=56 * 1024 * 1024
        ),
    )(
        queries.reshape(by_head),
        new_keys.reshape(own, steps * kv_heads, head_dim),
        new_values.reshape(own, steps * kv_heads, head_dim),
        lengths,
        prompt_keys.reshape(positions * groups, head_dim),
        prompt_values.reshape(positions * groups, head_dim),
        suffix_keys.reshape(own, suffix_rows, head_dim),
        suffix_values.reshape(own, suffix_rows, head_dim),
    )
    return result.reshape(own, steps, features)


def solution(mesh):
    return jax.shard_map(
        functools.partial(local, mesh.shape["ctx"], mesh.shape["dec"]),
        mesh=mesh,
        in_specs=(
            P(("ctx", "dec"), None, None),
            P("ctx", "dec", None),
            P("ctx", "dec", None),
            P(("ctx", "dec"), None, None, None),
            P(("ctx", "dec"), None, None, None),
            P(("ctx", "dec"), None, None, None),
            P(("ctx", "dec"), None, None, None),
            P(("ctx", "dec")),
        ),
        out_specs=P(("ctx", "dec"), None, None),
        check_vma=False,
    )
```

```python
import functools

import jax
import jax.numpy as jnp
from jax import lax
from jax.experimental import pallas as pl
from jax.experimental.pallas import tpu as pltpu
from jax.sharding import PartitionSpec as P

MESH = pl.DeviceIdType.MESH
MASKED_SCORE = -1e30
FLOOR = -1e29
LOG2E = 1.4426950408889634
F32 = jnp.float32
BF16 = jnp.bfloat16
NT = (((1,), (1,)), ((), ()))


def dot_nt(left, right):
    return lax.dot_general(left, right, NT, preferred_element_type=F32)


def dot(left, right):
    return jnp.dot(left, right, preferred_element_type=F32)


def kernel(
    sizes,
    q_flat,
    nk_ref,
    nv_ref,
    len_ref,
    pk_hbm,
    pv_hbm,
    sk_hbm,
    sv_hbm,
    out_ref,
    pk_raw,
    pv_raw,
    sk,
    sv,
    keys,
    values_t,
    q_ref,
    qbuf,
    own_o,
    own_s,
    xo_send,
    xs_send,
    xo_recv,
    xs_recv,
    zo_send,
    zs_send,
    zo_recv,
    zs_recv,
    fo,
    fs,
    po_recv,
    ps_recv,
    stat_rows,
    suf_o,
    suf_m,
    suf_l,
    load_sem,
    g1_send,
    g1_recv,
    g2_send,
    g2_recv,
    gx_send,
    gx_recv,
    xo_sem,
    xs_sem,
    zo_sem,
    zs_sem,
    po_sem,
    ps_sem,
):
    ctx_n, dec_n, groups, rows, head_dim, kv_heads, per_group, steps, own = sizes
    pairs = ctx_n // 2
    unit = dec_n * rows
    positions = keys.shape[1]
    suffix_rows = sk.shape[1]
    scale = head_dim ** (-0.5) * LOG2E
    c = lax.axis_index("ctx")
    d = lax.axis_index("dec")
    z = c // 2
    x = c % 2

    def at_z(j, half):
        other = lax.bitwise_xor(z, jnp.int32(j))
        return other * 2 + (x if half == 0 else 1 - x)

    def dec_of(j):
        return lax.bitwise_xor(d, jnp.int32(j))

    loads = []
    for i, (src, dst) in enumerate(((pk_hbm, pk_raw), (pv_hbm, pv_raw))):
        loads.append(pltpu.make_async_copy(src, dst, load_sem.at[i]))
    for s in range(own):
        for i, (src, dst) in enumerate(((sk_hbm, sk), (sv_hbm, sv))):
            loads.append(pltpu.make_async_copy(src.at[s], dst.at[s], load_sem.at[2 + 2 * s + i]))
    for load in loads:
        load.start()

    barrier = pltpu.get_barrier_semaphore()
    partners = [(c, dec_of(j)) for j in range(1, dec_n)]
    partners += [(at_z(j, 0), d) for j in range(1, pairs)]
    partners += [(at_z(0, 1), d)]
    for partner in partners:
        pl.semaphore_signal(barrier, inc=1, device_id=partner, device_id_type=MESH)
    for s in range(own):
        wide = q_flat[s].astype(F32)
        for t in range(steps):
            for h in range(kv_heads):
                first = h * per_group
                q_ref[s, t, h // groups, h % groups] = jnp.concatenate(
                    [wide[t:t + 1, (first + i) * head_dim:(first + i + 1) * head_dim]
                     for i in range(per_group)], axis=0).astype(BF16)
    pl.semaphore_wait(barrier, len(partners))

    def remote(src, dst, send_sem, recv_sem, target):
        return pltpu.make_async_remote_copy(
            src_ref=src, dst_ref=dst, send_sem=send_sem, recv_sem=recv_sem,
            device_id=target, device_id_type=MESH,
        )

    span = 256 // groups
    perm_r = lax.broadcasted_iota(jnp.int32, (256, 256), 0)
    perm_i = lax.broadcasted_iota(jnp.int32, (256, 256), 1)
    perm = ((perm_r % span) * groups + perm_r // span == perm_i).astype(BF16)
    eye = (lax.broadcasted_iota(jnp.int32, (head_dim, head_dim), 0)
           == lax.broadcasted_iota(jnp.int32, (head_dim, head_dim), 1)).astype(BF16)

    def prepare_keys(raw, there):
        key_rows = dot(perm, pk_raw[raw, :]).astype(BF16)
        for g in range(groups):
            keys[g, there, :] = key_rows[g * span:(g + 1) * span]

    def prepare_values(raw, there):
        value_rows = dot(perm, pv_raw[raw, :]).astype(BF16)
        turned = dot_nt(eye, value_rows).astype(BF16)
        for g in range(groups):
            values_t[g, :head_dim, there] = turned[:, g * span:(g + 1) * span]

    def prepare_all(prepare):
        count = positions * groups // 256
        at_once = 8

        def step(i, carry):
            for k in range(at_once):
                b = i * at_once + k
                prepare(pl.ds(pl.multiple_of(b * 256, 256), 256),
                        pl.ds(pl.multiple_of(b * span, span), span))
            return carry

        lax.fori_loop(0, count // at_once, step, 0)

    own_rows = pl.ds(pl.multiple_of(d * rows, rows), rows)
    g1 = []
    for j in range(1, dec_n):
        copy = remote(q_ref.at[:, :, dec_of(j)], qbuf.at[c, d],
                      g1_send.at[j], g1_recv.at[j], (c, dec_of(j)))
        copy.start()
        g1.append(copy)
    qbuf[c, d] = q_ref[:, :, d]
    loads[0].wait()
    prepare_all(prepare_keys)
    for copy in g1:
        copy.wait()
    g2 = {}
    for j in range(1, pairs):
        g2[j] = remote(qbuf.at[c], qbuf.at[c], g2_send.at[j], g2_recv.at[j], (at_z(j, 0), d))
        g2[j].start()
    gx = {}

    def forward(j):
        if j:
            g2[j].wait_recv()
        here = at_z(j, 0)
        gx[j] = remote(qbuf.at[here], qbuf.at[here], gx_send.at[j], gx_recv.at[j], (at_z(0, 1), d))
        gx[j].start()

    forward(0)

    loads[1].wait()
    prepare_all(prepare_values)
    values_t[:, head_dim:, :] = jnp.ones_like(values_t[:, head_dim:, :])

    chunk = min(512, suffix_rows // kv_heads) * kv_heads
    per_step = kv_heads * per_group
    q_rows = steps * per_step
    per_row = steps * per_group
    lane_head = lax.broadcasted_iota(jnp.int32, (per_group, head_dim), 1) % kv_heads
    hits = [lane_head == g for g in range(kv_heads)]
    lane_place = lax.broadcasted_iota(jnp.int32, (per_row, head_dim), 1) // kv_heads

    def around(op, folded):
        shift = kv_heads
        while shift < head_dim:
            folded = op(folded, pltpu.roll(folded, shift, 1))
            shift *= 2
        return folded

    def by_row(folded):
        return jnp.concatenate(
            [folded[t * per_group:(t + 1) * per_group, g:g + 1]
             for t in range(steps) for g in range(kv_heads)], axis=0)

    def suffix_query(s):
        return q_ref[s].astype(F32).reshape(q_rows, head_dim).astype(BF16)

    def suffix_merge(left, right):
        top = jnp.maximum(left[0], right[0])
        a = jnp.exp2((left[0] - top) * scale)
        b = jnp.exp2((right[0] - top) * scale)
        return top, left[1] * a + right[1] * b, left[2] * a + right[2] * b

    def suffix_new(s):
        q = suffix_query(s)
        new_rows = steps * kv_heads
        col = lax.broadcasted_iota(jnp.int32, (q_rows, new_rows), 1)
        row = lax.broadcasted_iota(jnp.int32, (q_rows, new_rows), 0)
        seen = (col % kv_heads == row // per_group % kv_heads) & (col // kv_heads <= row // per_step)
        masked = jnp.where(seen, dot_nt(q, nk_ref[s]), MASKED_SCORE)
        top = jnp.max(masked, axis=1, keepdims=True)
        weights = jnp.exp2((masked - top) * scale).astype(BF16)
        return top, jnp.sum(weights.astype(F32), axis=1, keepdims=True), dot(weights, nv_ref[s])

    def suffix_part(s, b):
        here = slice(b * chunk, (b + 1) * chunk)
        scores = dot_nt(suffix_query(s), sk[s, here, :])
        left = len_ref[s] - b * (chunk // kv_heads)
        found = []
        for k in range(chunk // head_dim):
            lanes = slice(k * head_dim, (k + 1) * head_dim)
            picked = []
            for t in range(steps):
                base = t * per_step
                one = scores[base:base + per_group, lanes]
                for g in range(1, kv_heads):
                    first = base + g * per_group
                    one = jnp.where(hits[g], scores[first:first + per_group, lanes], one)
                picked.append(one)
            visible = lane_place < left - k * (head_dim // kv_heads)
            found.append(jnp.where(visible, jnp.concatenate(picked, axis=0), MASKED_SCORE))
        top = jnp.maximum(around(jnp.maximum, functools.reduce(jnp.maximum, found)), FLOOR)
        total = 0.0
        spread = []
        for one in found:
            weights = jnp.exp2((one - top) * scale).astype(BF16).astype(F32)
            total = total + weights
            spread.append(jnp.concatenate(
                [jnp.where(hits[g], weights[t * per_group:(t + 1) * per_group], 0.0)
                 for t in range(steps) for g in range(kv_heads)], axis=0).astype(BF16))
        summed = dot(jnp.concatenate(spread, axis=1), sv[s, here, :])
        return by_row(top), by_row(around(jnp.add, total)), summed

    def suffix_store(s, state):
        for t in range(steps):
            for g in range(kv_heads):
                first = t * per_step + g * per_group
                rows_here = slice(first, first + per_group)
                mine = slice(s * per_row + t * per_group, s * per_row + (t + 1) * per_group)
                shape = (per_group, head_dim)
                suf_o[g, mine, :] = state[2][rows_here]
                suf_l[g, mine, :] = jnp.broadcast_to(state[1][rows_here], shape)
                suf_m[g, mine, :] = jnp.broadcast_to(state[0][rows_here] * scale, shape)

    suffix_blocks = suffix_rows // chunk
    pieces = [(s, b) for s in range(own) for b in range(suffix_blocks)]
    states = {}

    def suffix(many):
        for _ in range(min(many, len(pieces))):
            s, b = pieces.pop(0)
            if b == 0:
                states[s] = suffix_new(s)
                loads[2 + 2 * s].wait()
                loads[3 + 2 * s].wait()
            states[s] = suffix_merge(states[s], suffix_part(s, b))
            if b == suffix_blocks - 1:
                suffix_store(s, states[s])

    suffix(max(1, len(pieces) - 3))

    block = min(512, positions)

    def tile(j):
        mine, theirs = at_z(j, 0), at_z(j, 1)

        stages = [(g, b) for g in range(groups) for b in range(positions // block)]
        queries, tops, sums = {}, {}, {}
        for g in range(groups):
            queries[g] = jnp.concatenate(
                [qbuf[at, :, :, :, g].astype(F32).reshape(unit, head_dim) for at in (mine, theirs)],
                axis=0).astype(BF16)
            tops[g], sums[g] = [], []

        def score(g, b):
            return dot_nt(keys[g, b * block:(b + 1) * block, :], queries[g])

        def value(g, b, weights):
            sums[g].append(dot(values_t[g, :, b * block:(b + 1) * block], weights))

        def finish(g):
            top = functools.reduce(jnp.maximum, tops[g])
            total = sum(one * jnp.exp2(m - top) for one, m in zip(sums[g], tops[g]))
            stats = jnp.concatenate([
                jnp.broadcast_to(top, (4, 2 * unit)), total[head_dim:head_dim + 4]], axis=0)
            total = total[:head_dim]
            own_o[j, g] = total[:, :unit]
            own_s[j, g] = stats[:, :unit]
            xo_send[j, g] = total[:, unit:].astype(BF16)
            xs_send[j, g] = stats[:, unit:]

        scores = score(*stages[0])
        waiting = None
        for i, (g, b) in enumerate(stages):
            following = score(*stages[i + 1]) if i + 1 < len(stages) else None
            if waiting is not None:
                value(*waiting)
            top = jnp.max(scores, axis=0, keepdims=True)
            tops[g].append(top * scale)
            waiting = (g, b, jnp.exp2((scores - top) * scale).astype(BF16))
            scores = following
            if b == 0 and g:
                finish(g - 1)
        value(*waiting)
        finish(groups - 1)

    xs = {}
    zs = {}

    def send_x(j):
        target = (at_z(0, 1), d)
        xs[j] = (
            remote(xo_send.at[j], xo_recv.at[j], xo_sem.at[0, j], xo_sem.at[1, j], target),
            remote(xs_send.at[j], xs_recv.at[j], xs_sem.at[0, j], xs_sem.at[1, j], target),
        )
        for copy in xs[j]:
            copy.start()

    def merged(parts):
        top = functools.reduce(jnp.maximum, [stats[0:1] for _, stats in parts])
        total, weight = 0.0, 0.0
        for sums, stats in parts:
            factor = jnp.exp2(stats[0:1] - top)
            total = total + sums.astype(F32) * factor
            weight = weight + stats[4:5] * factor
        width = top.shape[1]
        return total, jnp.concatenate(
            [jnp.broadcast_to(top, (4, width)), jnp.broadcast_to(weight, (4, width))], axis=0)

    def merge_x(j):
        for copy in xs[j]:
            copy.wait_recv()
        for g in range(groups):
            total, stats = merged([(own_o[j, g], own_s[j, g]), (xo_recv[j, g], xs_recv[j, g])])
            if j:
                zo_send[j, g] = total.astype(BF16)
                zs_send[j, g] = stats
            else:
                own_o[j, g] = total
                own_s[j, g] = stats
        if j:
            target = (at_z(j, 0), d)
            zs[j] = (
                remote(zo_send.at[j], zo_recv.at[j], zo_sem.at[0, j], zo_sem.at[1, j], target),
                remote(zs_send.at[j], zs_recv.at[j], zs_sem.at[0, j], zs_sem.at[1, j], target),
            )
            for copy in zs[j]:
                copy.start()

    for j in range(pairs):
        if j + 1 < pairs:
            forward(j + 1)
        gx[j].wait_recv()
        tile(j)
        send_x(j)
        if j:
            merge_x(j - 1)
    suffix(1)
    merge_x(pairs - 1)
    suffix(1)

    for j in range(1, pairs):
        for copy in zs[j]:
            copy.wait_recv()
    for g in range(groups):
        total, stats = merged([(own_o[0, g], own_s[0, g])]
                              + [(zo_recv[j, g], zs_recv[j, g]) for j in range(1, pairs)])
        fo[g] = total.T.astype(BF16)
        fs[g] = stats
    ps = []
    for j in range(1, dec_n):
        target = dec_of(j)
        there = pl.ds(pl.multiple_of(target * rows, rows), rows)
        ps.append(remote(fo.at[:, there, :], po_recv.at[d], po_sem.at[0, j], po_sem.at[1, j],
                         (c, target)))
        ps.append(remote(fs, ps_recv.at[d], ps_sem.at[0, j], ps_sem.at[1, j], (c, target)))
    for copy in ps:
        copy.start()
    po_recv[d] = fo[:, own_rows, :]
    ps_recv[d] = fs[...]
    suffix(len(pieces))
    for copy in ps:
        copy.wait_recv()
    flat = ps_recv[...].reshape(kv_heads * 8, unit)
    stat_rows[...] = flat.T
    picked = stat_rows[own_rows, :]
    results = []
    for h in range(kv_heads):
        top_p = picked[:, h * 8:h * 8 + 1]
        sum_p = picked[:, h * 8 + 4:h * 8 + 5]
        top = jnp.maximum(top_p, suf_m[h])
        left = jnp.exp2(top_p - top)
        right = jnp.exp2(suf_m[h] - top)
        prompt = po_recv[h // groups, h % groups].astype(F32)
        results.append((prompt * left + suf_o[h] * right) / (sum_p * left + suf_l[h] * right))
    for s in range(own):
        out_ref[s] = jnp.concatenate(
            [jnp.concatenate(
                [one[first:first + 1] for first in
                 range(s * per_row + i, (s + 1) * per_row, per_group)], axis=0)
             for one in results for i in range(per_group)], axis=1).astype(BF16)

    for copy in list(g2.values()) + list(gx.values()):
        copy.wait_send()
    for both in list(xs.values()) + list(zs.values()):
        for copy in both:
            copy.wait_send()
    for copy in ps:
        copy.wait_send()


def local(ctx_n, dec_n, queries, prompt_keys, prompt_values, suffix_keys, suffix_values,
          new_keys, new_values, lengths):
    own, steps, features = queries.shape
    positions, groups, head_dim = prompt_keys.shape
    suffix_length, kv_heads = suffix_keys.shape[1:3]
    per_group = features // (kv_heads * head_dim)
    rows = own * steps * per_group
    unit = dec_n * rows
    pairs = ctx_n // 2
    by_head = (own, steps, dec_n, groups, per_group, head_dim)
    suffix_rows = suffix_length * kv_heads
    sizes = (ctx_n, dec_n, groups, rows, head_dim, kv_heads, per_group, steps, own)
    vmem = pl.BlockSpec(memory_space=pltpu.VMEM)
    anywhere = pl.BlockSpec(memory_space=pl.ANY)
    dma = pltpu.SemaphoreType.DMA
    moved = (pairs, groups, head_dim, unit)
    noted = (pairs, groups, 8, unit)
    return pl.pallas_call(
        functools.partial(kernel, sizes),
        out_shape=jax.ShapeDtypeStruct((own, steps, features), BF16),
        in_specs=[vmem, vmem, vmem, pl.BlockSpec(memory_space=pltpu.SMEM)] + [anywhere] * 4,
        out_specs=vmem,
        scratch_shapes=[
            pltpu.VMEM((positions * groups, head_dim), BF16),
            pltpu.VMEM((positions * groups, head_dim), BF16),
            pltpu.VMEM((own, suffix_rows, head_dim), BF16),
            pltpu.VMEM((own, suffix_rows, head_dim), BF16),
            pltpu.VMEM((groups, positions, head_dim), BF16),
            pltpu.VMEM((groups, head_dim + 16, positions), BF16),
            pltpu.VMEM(by_head, BF16),
            pltpu.VMEM((ctx_n, dec_n, own, steps, groups, per_group, head_dim), BF16),
            pltpu.VMEM(moved, F32),
            pltpu.VMEM(noted, F32),
            pltpu.VMEM(moved, BF16),
            pltpu.VMEM(noted, F32),
            pltpu.VMEM(moved, BF16),
            pltpu.VMEM(noted, F32),
            pltpu.VMEM(moved, BF16),
            pltpu.VMEM(noted, F32),
            pltpu.VMEM(moved, BF16),
            pltpu.VMEM(noted, F32),
            pltpu.VMEM((groups, unit, head_dim), BF16),
            pltpu.VMEM((groups, 8, unit), F32),
            pltpu.VMEM((dec_n, groups, rows, head_dim), BF16),
            pltpu.VMEM((dec_n, groups, 8, unit), F32),
            pltpu.VMEM((unit, kv_heads * 8), F32),
            pltpu.VMEM((kv_heads, rows, head_dim), F32),
            pltpu.VMEM((kv_heads, rows, head_dim), F32),
            pltpu.VMEM((kv_heads, rows, head_dim), F32),
            dma((2 + 2 * own,)),
            dma((dec_n,)),
            dma((dec_n,)),
            dma((pairs,)),
            dma((pairs,)),
            dma((pairs,)),
            dma((pairs,)),
            dma((2, pairs)),
            dma((2, pairs)),
            dma((2, pairs)),
            dma((2, pairs)),
            dma((2, dec_n)),
            dma((2, dec_n)),
        ],
        compiler_params=pltpu.CompilerParams(
            collective_id=0, has_side_effects=True, vmem_limit_bytes=56 * 1024 * 1024
        ),
    )(
        queries,
        new_keys.reshape(own, steps * kv_heads, head_dim),
        new_values.reshape(own, steps * kv_heads, head_dim),
        lengths,
        prompt_keys.reshape(positions * groups, head_dim),
        prompt_values.reshape(positions * groups, head_dim),
        suffix_keys.reshape(own, suffix_rows, head_dim),
        suffix_values.reshape(own, suffix_rows, head_dim),
    )

def solution(mesh):
    return jax.shard_map(
        functools.partial(local, mesh.shape["ctx"], mesh.shape["dec"]),
        mesh=mesh,
        in_specs=(
            P(("ctx", "dec"), None, None),
            P("ctx", "dec", None),
            P("ctx", "dec", None),
            P(("ctx", "dec"), None, None, None),
            P(("ctx", "dec"), None, None, None),
            P(("ctx", "dec"), None, None, None),
            P(("ctx", "dec"), None, None, None),
            P(("ctx", "dec")),
        ),
        out_specs=P(("ctx", "dec"), None, None),
        check_vma=False,
    )
```

```python
import functools

import jax
import jax.numpy as jnp
from jax import lax
from jax.experimental import pallas as pl
from jax.experimental.pallas import tpu as pltpu
from jax.sharding import PartitionSpec as P

MESH = pl.DeviceIdType.MESH
MASKED_SCORE = -1e30
FLOOR = -1e29
LOG2E = 1.4426950408889634
F32 = jnp.float32
BF16 = jnp.bfloat16
NT = (((1,), (1,)), ((), ()))


def dot_nt(left, right):
    return lax.dot_general(left, right, NT, preferred_element_type=F32)


def dot(left, right):
    return jnp.dot(left, right, preferred_element_type=F32)


def kernel(
    sizes,
    q_flat,
    nk_ref,
    nv_ref,
    len_ref,
    pk_hbm,
    pv_hbm,
    sk_hbm,
    sv_hbm,
    out_ref,
    pk_raw,
    pv_raw,
    sk,
    sv,
    keys,
    values_t,
    q_ref,
    qbuf,
    own_o,
    own_s,
    xo_send,
    xs_send,
    xo_recv,
    xs_recv,
    zo_send,
    zs_send,
    zo_recv,
    zs_recv,
    fo,
    fs,
    po_recv,
    ps_recv,
    stat_rows,
    suf_o,
    suf_m,
    suf_l,
    load_sem,
    g1_send,
    g1_recv,
    g2_send,
    g2_recv,
    gx_send,
    gx_recv,
    xo_sem,
    xs_sem,
    zo_sem,
    zs_sem,
    po_sem,
    ps_sem,
):
    ctx_n, dec_n, groups, rows, head_dim, kv_heads, per_group, steps, own = sizes
    pairs = ctx_n // 2
    unit = dec_n * rows
    positions = keys.shape[1]
    suffix_rows = sk.shape[1]
    scale = head_dim ** (-0.5) * LOG2E
    c = lax.axis_index("ctx")
    d = lax.axis_index("dec")
    z = c // 2
    x = c % 2

    def at_z(j, half):
        other = lax.bitwise_xor(z, jnp.int32(j))
        return other * 2 + (x if half == 0 else 1 - x)

    def dec_of(j):
        return lax.bitwise_xor(d, jnp.int32(j))

    loads = []
    for i, (src, dst) in enumerate(((pk_hbm, pk_raw), (pv_hbm, pv_raw))):
        loads.append(pltpu.make_async_copy(src, dst, load_sem.at[i]))
    for s in range(own):
        for i, (src, dst) in enumerate(((sk_hbm, sk), (sv_hbm, sv))):
            loads.append(pltpu.make_async_copy(src.at[s], dst.at[s], load_sem.at[2 + 2 * s + i]))
    for load in loads:
        load.start()

    barrier = pltpu.get_barrier_semaphore()
    partners = [(c, dec_of(j)) for j in range(1, dec_n)]
    partners += [(at_z(j, 0), d) for j in range(1, pairs)]
    partners += [(at_z(0, 1), d)]
    for partner in partners:
        pl.semaphore_signal(barrier, inc=1, device_id=partner, device_id_type=MESH)
    for s in range(own):
        wide = q_flat[s].astype(F32)
        for t in range(steps):
            for h in range(kv_heads):
                first = h * per_group
                q_ref[s, t, h // groups, h % groups] = jnp.concatenate(
                    [wide[t:t + 1, (first + i) * head_dim:(first + i + 1) * head_dim]
                     for i in range(per_group)], axis=0).astype(BF16)
    pl.semaphore_wait(barrier, len(partners))

    def remote(src, dst, send_sem, recv_sem, target):
        return pltpu.make_async_remote_copy(
            src_ref=src, dst_ref=dst, send_sem=send_sem, recv_sem=recv_sem,
            device_id=target, device_id_type=MESH,
        )

    span = 256 // groups
    perm_r = lax.broadcasted_iota(jnp.int32, (256, 256), 0)
    perm_i = lax.broadcasted_iota(jnp.int32, (256, 256), 1)
    perm = ((perm_r % span) * groups + perm_r // span == perm_i).astype(BF16)
    eye = (lax.broadcasted_iota(jnp.int32, (head_dim, head_dim), 0)
           == lax.broadcasted_iota(jnp.int32, (head_dim, head_dim), 1)).astype(BF16)

    def prepare_keys(raw, there):
        key_rows = dot(perm, pk_raw[raw, :]).astype(BF16)
        for g in range(groups):
            keys[g, there, :] = key_rows[g * span:(g + 1) * span]

    def prepare_values(raw, there):
        value_rows = dot(perm, pv_raw[raw, :]).astype(BF16)
        turned = dot_nt(eye, value_rows).astype(BF16)
        for g in range(groups):
            values_t[g, :head_dim, there] = turned[:, g * span:(g + 1) * span]

    at_once = min(8, positions * groups // 256)
    prepare_steps = positions * groups // 256 // at_once

    def prepare_all(prepare, first, last):

        def step(i, carry):
            for k in range(at_once):
                b = i * at_once + k
                prepare(pl.ds(pl.multiple_of(b * 256, 256), 256),
                        pl.ds(pl.multiple_of(b * span, span), span))
            return carry

        lax.fori_loop(first, last, step, 0)

    own_rows = pl.ds(pl.multiple_of(d * rows, rows), rows)
    g1 = []
    for j in range(1, dec_n):
        copy = remote(q_ref.at[:, :, dec_of(j)], qbuf.at[c, d],
                      g1_send.at[j], g1_recv.at[j], (c, dec_of(j)))
        copy.start()
        g1.append(copy)
    qbuf[c, d] = q_ref[:, :, d]
    loads[0].wait()
    prepare_all(prepare_keys, 0, prepare_steps // 2)
    for copy in g1:
        copy.wait()
    g2 = {}
    for j in range(1, pairs):
        g2[j] = remote(qbuf.at[c], qbuf.at[c], g2_send.at[j], g2_recv.at[j], (at_z(j, 0), d))
        g2[j].start()
    gx = {}

    def forward(j):
        if j:
            g2[j].wait_recv()
        here = at_z(j, 0)
        gx[j] = remote(qbuf.at[here], qbuf.at[here], gx_send.at[j], gx_recv.at[j], (at_z(0, 1), d))
        gx[j].start()

    forward(0)

    loads[1].wait()
    prepare_all(prepare_keys, prepare_steps // 2, prepare_steps)
    prepare_all(prepare_values, 0, prepare_steps)
    values_t[:, head_dim:, :] = jnp.ones_like(values_t[:, head_dim:, :])

    chunk = min(512, suffix_rows // kv_heads) * kv_heads
    per_step = kv_heads * per_group
    q_rows = steps * per_step
    per_row = steps * per_group
    lane_head = lax.broadcasted_iota(jnp.int32, (per_group, head_dim), 1) % kv_heads
    hits = [lane_head == g for g in range(kv_heads)]
    lane_place = lax.broadcasted_iota(jnp.int32, (per_row, head_dim), 1) // kv_heads

    def around(op, folded):
        shift = kv_heads
        while shift < head_dim:
            folded = op(folded, pltpu.roll(folded, shift, 1))
            shift *= 2
        return folded

    def by_row(folded):
        return jnp.concatenate(
            [folded[t * per_group:(t + 1) * per_group, g:g + 1]
             for t in range(steps) for g in range(kv_heads)], axis=0)

    def suffix_query(s):
        return q_ref[s].astype(F32).reshape(q_rows, head_dim).astype(BF16)

    def suffix_merge(left, right):
        top = jnp.maximum(left[0], right[0])
        a = jnp.exp2((left[0] - top) * scale)
        b = jnp.exp2((right[0] - top) * scale)
        return top, left[1] * a + right[1] * b, left[2] * a + right[2] * b

    def suffix_new(s):
        q = suffix_query(s)
        new_rows = steps * kv_heads
        col = lax.broadcasted_iota(jnp.int32, (q_rows, new_rows), 1)
        row = lax.broadcasted_iota(jnp.int32, (q_rows, new_rows), 0)
        seen = (col % kv_heads == row // per_group % kv_heads) & (col // kv_heads <= row // per_step)
        masked = jnp.where(seen, dot_nt(q, nk_ref[s]), MASKED_SCORE)
        top = jnp.max(masked, axis=1, keepdims=True)
        weights = jnp.exp2((masked - top) * scale).astype(BF16)
        return top, jnp.sum(weights.astype(F32), axis=1, keepdims=True), dot(weights, nv_ref[s])

    def suffix_part(s, b):
        here = slice(b * chunk, (b + 1) * chunk)
        scores = dot_nt(suffix_query(s), sk[s, here, :])
        left = len_ref[s] - b * (chunk // kv_heads)
        found = []
        for k in range(chunk // head_dim):
            lanes = slice(k * head_dim, (k + 1) * head_dim)
            picked = []
            for t in range(steps):
                base = t * per_step
                one = scores[base:base + per_group, lanes]
                for g in range(1, kv_heads):
                    first = base + g * per_group
                    one = jnp.where(hits[g], scores[first:first + per_group, lanes], one)
                picked.append(one)
            visible = lane_place < left - k * (head_dim // kv_heads)
            found.append(jnp.where(visible, jnp.concatenate(picked, axis=0), MASKED_SCORE))
        top = jnp.maximum(around(jnp.maximum, functools.reduce(jnp.maximum, found)), FLOOR)
        total = 0.0
        spread = []
        for one in found:
            weights = jnp.exp2((one - top) * scale).astype(BF16).astype(F32)
            total = total + weights
            spread.append(jnp.concatenate(
                [jnp.where(hits[g], weights[t * per_group:(t + 1) * per_group], 0.0)
                 for t in range(steps) for g in range(kv_heads)], axis=0).astype(BF16))
        summed = dot(jnp.concatenate(spread, axis=1), sv[s, here, :])
        return by_row(top), by_row(around(jnp.add, total)), summed

    def suffix_store(s, state):
        for t in range(steps):
            for g in range(kv_heads):
                first = t * per_step + g * per_group
                rows_here = slice(first, first + per_group)
                mine = slice(s * per_row + t * per_group, s * per_row + (t + 1) * per_group)
                shape = (per_group, head_dim)
                suf_o[g, mine, :] = state[2][rows_here]
                suf_l[g, mine, :] = jnp.broadcast_to(state[1][rows_here], shape)
                suf_m[g, mine, :] = jnp.broadcast_to(state[0][rows_here] * scale, shape)

    suffix_blocks = suffix_rows // chunk
    pieces = [(s, b) for s in range(own) for b in range(suffix_blocks)]
    states = {}

    def suffix(many):
        for _ in range(min(many, len(pieces))):
            s, b = pieces.pop(0)
            if b == 0:
                states[s] = suffix_new(s)
                loads[2 + 2 * s].wait()
                loads[3 + 2 * s].wait()
            states[s] = suffix_merge(states[s], suffix_part(s, b))
            if b == suffix_blocks - 1:
                suffix_store(s, states[s])

    suffix(max(1, len(pieces) - 3))

    block = min(512, positions)

    def tile(j):
        mine, theirs = at_z(j, 0), at_z(j, 1)

        stages = [(g, b) for g in range(groups) for b in range(positions // block)]
        queries, tops, sums = {}, {}, {}
        for g in range(groups):
            queries[g] = jnp.concatenate(
                [qbuf[at, :, :, :, g].astype(F32).reshape(unit, head_dim) for at in (mine, theirs)],
                axis=0).astype(BF16)
            tops[g], sums[g] = [], []

        def score(g, b):
            return dot_nt(keys[g, b * block:(b + 1) * block, :], queries[g])

        def value(g, b, weights):
            sums[g].append(dot(values_t[g, :, b * block:(b + 1) * block], weights))

        def finish(g):
            top = functools.reduce(jnp.maximum, tops[g])
            total = sum(one * jnp.exp2(m - top) for one, m in zip(sums[g], tops[g]))
            stats = jnp.concatenate([
                jnp.broadcast_to(top, (4, 2 * unit)), total[head_dim:head_dim + 4]], axis=0)
            total = total[:head_dim]
            own_o[j, g] = total[:, :unit]
            own_s[j, g] = stats[:, :unit]
            xo_send[j, g] = total[:, unit:].astype(BF16)
            xs_send[j, g] = stats[:, unit:]

        scores = score(*stages[0])
        waiting = None
        for i, (g, b) in enumerate(stages):
            following = score(*stages[i + 1]) if i + 1 < len(stages) else None
            if waiting is not None:
                value(*waiting)
            top = jnp.max(scores, axis=0, keepdims=True)
            tops[g].append(top * scale)
            waiting = (g, b, jnp.exp2((scores - top) * scale).astype(BF16))
            scores = following
            if b == 0 and g:
                finish(g - 1)
        value(*waiting)
        finish(groups - 1)

    xs = {}
    zs = {}

    def send_x(j):
        target = (at_z(0, 1), d)
        xs[j] = (
            remote(xo_send.at[j], xo_recv.at[j], xo_sem.at[0, j], xo_sem.at[1, j], target),
            remote(xs_send.at[j], xs_recv.at[j], xs_sem.at[0, j], xs_sem.at[1, j], target),
        )
        for copy in xs[j]:
            copy.start()

    def merged(parts):
        top = functools.reduce(jnp.maximum, [stats[0:1] for _, stats in parts])
        total, weight = 0.0, 0.0
        for sums, stats in parts:
            factor = jnp.exp2(stats[0:1] - top)
            total = total + sums.astype(F32) * factor
            weight = weight + stats[4:5] * factor
        width = top.shape[1]
        return total, jnp.concatenate(
            [jnp.broadcast_to(top, (4, width)), jnp.broadcast_to(weight, (4, width))], axis=0)

    def merge_x(j):
        for copy in xs[j]:
            copy.wait_recv()
        for g in range(groups):
            total, stats = merged([(own_o[j, g], own_s[j, g]), (xo_recv[j, g], xs_recv[j, g])])
            if j:
                zo_send[j, g] = total.astype(BF16)
                zs_send[j, g] = stats
            else:
                own_o[j, g] = total
                own_s[j, g] = stats
        if j:
            target = (at_z(j, 0), d)
            zs[j] = (
                remote(zo_send.at[j], zo_recv.at[j], zo_sem.at[0, j], zo_sem.at[1, j], target),
                remote(zs_send.at[j], zs_recv.at[j], zs_sem.at[0, j], zs_sem.at[1, j], target),
            )
            for copy in zs[j]:
                copy.start()

    for j in range(pairs):
        if j + 1 < pairs:
            forward(j + 1)
        gx[j].wait_recv()
        tile(j)
        send_x(j)
        if j:
            merge_x(j - 1)
    suffix(1)
    merge_x(pairs - 1)
    suffix(1)

    for j in range(1, pairs):
        for copy in zs[j]:
            copy.wait_recv()
    for g in range(groups):
        total, stats = merged([(own_o[0, g], own_s[0, g])]
                              + [(zo_recv[j, g], zs_recv[j, g]) for j in range(1, pairs)])
        fo[g] = total.T.astype(BF16)
        fs[g] = stats
    ps = []
    for j in range(1, dec_n):
        target = dec_of(j)
        there = pl.ds(pl.multiple_of(target * rows, rows), rows)
        ps.append(remote(fo.at[:, there, :], po_recv.at[d], po_sem.at[0, j], po_sem.at[1, j],
                         (c, target)))
        ps.append(remote(fs, ps_recv.at[d], ps_sem.at[0, j], ps_sem.at[1, j], (c, target)))
    for copy in ps:
        copy.start()
    po_recv[d] = fo[:, own_rows, :]
    ps_recv[d] = fs[...]
    suffix(len(pieces))
    for copy in ps:
        copy.wait_recv()
    flat = ps_recv[...].reshape(kv_heads * 8, unit)
    stat_rows[...] = flat.T
    picked = stat_rows[own_rows, :]
    results = []
    for h in range(kv_heads):
        top_p = picked[:, h * 8:h * 8 + 1]
        sum_p = picked[:, h * 8 + 4:h * 8 + 5]
        top = jnp.maximum(top_p, suf_m[h])
        left = jnp.exp2(top_p - top)
        right = jnp.exp2(suf_m[h] - top)
        prompt = po_recv[h // groups, h % groups].astype(F32)
        results.append((prompt * left + suf_o[h] * right) / (sum_p * left + suf_l[h] * right))
    for s in range(own):
        out_ref[s] = jnp.concatenate(
            [jnp.concatenate(
                [one[first:first + 1] for first in
                 range(s * per_row + i, (s + 1) * per_row, per_group)], axis=0)
             for one in results for i in range(per_group)], axis=1).astype(BF16)

    for copy in list(g2.values()) + list(gx.values()):
        copy.wait_send()
    for both in list(xs.values()) + list(zs.values()):
        for copy in both:
            copy.wait_send()
    for copy in ps:
        copy.wait_send()


def local(ctx_n, dec_n, queries, prompt_keys, prompt_values, suffix_keys, suffix_values,
          new_keys, new_values, lengths):
    own, steps, features = queries.shape
    positions, groups, head_dim = prompt_keys.shape
    suffix_length, kv_heads = suffix_keys.shape[1:3]
    per_group = features // (kv_heads * head_dim)
    rows = own * steps * per_group
    unit = dec_n * rows
    pairs = ctx_n // 2
    by_head = (own, steps, dec_n, groups, per_group, head_dim)
    suffix_rows = suffix_length * kv_heads
    sizes = (ctx_n, dec_n, groups, rows, head_dim, kv_heads, per_group, steps, own)
    vmem = pl.BlockSpec(memory_space=pltpu.VMEM)
    anywhere = pl.BlockSpec(memory_space=pl.ANY)
    dma = pltpu.SemaphoreType.DMA
    moved = (pairs, groups, head_dim, unit)
    noted = (pairs, groups, 8, unit)
    return pl.pallas_call(
        functools.partial(kernel, sizes),
        out_shape=jax.ShapeDtypeStruct((own, steps, features), BF16),
        in_specs=[vmem, vmem, vmem, pl.BlockSpec(memory_space=pltpu.SMEM)] + [anywhere] * 4,
        out_specs=vmem,
        scratch_shapes=[
            pltpu.VMEM((positions * groups, head_dim), BF16),
            pltpu.VMEM((positions * groups, head_dim), BF16),
            pltpu.VMEM((own, suffix_rows, head_dim), BF16),
            pltpu.VMEM((own, suffix_rows, head_dim), BF16),
            pltpu.VMEM((groups, positions, head_dim), BF16),
            pltpu.VMEM((groups, head_dim + 16, positions), BF16),
            pltpu.VMEM(by_head, BF16),
            pltpu.VMEM((ctx_n, dec_n, own, steps, groups, per_group, head_dim), BF16),
            pltpu.VMEM(moved, F32),
            pltpu.VMEM(noted, F32),
            pltpu.VMEM(moved, BF16),
            pltpu.VMEM(noted, F32),
            pltpu.VMEM(moved, BF16),
            pltpu.VMEM(noted, F32),
            pltpu.VMEM(moved, BF16),
            pltpu.VMEM(noted, F32),
            pltpu.VMEM(moved, BF16),
            pltpu.VMEM(noted, F32),
            pltpu.VMEM((groups, unit, head_dim), BF16),
            pltpu.VMEM((groups, 8, unit), F32),
            pltpu.VMEM((dec_n, groups, rows, head_dim), BF16),
            pltpu.VMEM((dec_n, groups, 8, unit), F32),
            pltpu.VMEM((unit, kv_heads * 8), F32),
            pltpu.VMEM((kv_heads, rows, head_dim), F32),
            pltpu.VMEM((kv_heads, rows, head_dim), F32),
            pltpu.VMEM((kv_heads, rows, head_dim), F32),
            dma((2 + 2 * own,)),
            dma((dec_n,)),
            dma((dec_n,)),
            dma((pairs,)),
            dma((pairs,)),
            dma((pairs,)),
            dma((pairs,)),
            dma((2, pairs)),
            dma((2, pairs)),
            dma((2, pairs)),
            dma((2, pairs)),
            dma((2, dec_n)),
            dma((2, dec_n)),
        ],
        compiler_params=pltpu.CompilerParams(
            collective_id=0, has_side_effects=True, vmem_limit_bytes=56 * 1024 * 1024
        ),
    )(
        queries,
        new_keys.reshape(own, steps * kv_heads, head_dim),
        new_values.reshape(own, steps * kv_heads, head_dim),
        lengths,
        prompt_keys.reshape(positions * groups, head_dim),
        prompt_values.reshape(positions * groups, head_dim),
        suffix_keys.reshape(own, suffix_rows, head_dim),
        suffix_values.reshape(own, suffix_rows, head_dim),
    )

def solution(mesh):
    return jax.shard_map(
        functools.partial(local, mesh.shape["ctx"], mesh.shape["dec"]),
        mesh=mesh,
        in_specs=(
            P(("ctx", "dec"), None, None),
            P("ctx", "dec", None),
            P("ctx", "dec", None),
            P(("ctx", "dec"), None, None, None),
            P(("ctx", "dec"), None, None, None),
            P(("ctx", "dec"), None, None, None),
            P(("ctx", "dec"), None, None, None),
            P(("ctx", "dec")),
        ),
        out_specs=P(("ctx", "dec"), None, None),
        check_vma=False,
    )
```
